32 devices in a mesh: clips: 2 (over y), frame: 4 (over x, core), row: 4 (over z).
Axes of the slice: x: 2, y: 2, z: 4, core: 2. Of those that a mesh axis runs over, the one named last changes fastest.
Arguments:
- frames: bfloat16 [16, 512, 640], P(('clips', 'frame'), 'row'), parts along dimension 0, may hold values from -16 to 16
- key_index: int32 [4], P('clips'), parts along dimension 0, may hold values from 0 to 7, as said below
- w_query: bfloat16 [640, 640], replicated, may hold values from -0.25 to 0.25
- w_keyval: bfloat16 [640, 1280], replicated, may hold values from -0.25 to 0.25
- w_out: bfloat16 [640, 640], replicated, may hold values from -0.25 to 0.25
- norm_gain: float32 [640], replicated, may hold values from 0.1 to 1.9
- w_first: bfloat16 [3, 640, 640], replicated, may hold values from -0.125 to 0.125
- w_second: bfloat16 [3, 640, 640], replicated, may hold values from -0.125 to 0.125
Outputs:
- edited: bfloat16 [16, 512, 640], P(('clips', 'frame'), 'row'), parts along dimension 0
The draws below stay inside these ranges and needn't reach their ends.
There are 2 independent parts, one for each index of `clips`. The reference program is written for one: setup_inputs(seed, part) draws one part's arguments, and reference() takes and returns one part's arrays. A program takes and returns all parts, laid end to end along the dimension named above; an argument that names none is the same for every part. Nothing has to cross between parts.
Inputs may be any that keep to these rules, and one draw needn't show every extreme that they name: `key_index`: two different frame indices of the window, in either order; one of them is the window's last frame 8 - 1.
All inputs are finite; a program needn't handle non-finite values.
Results may differ from the reference program's by a relative error of at most 0.0067.
Values may be sent and summed in bfloat16 or wider, within the bound.
A program may use at most 128 MiB of HBM per device.

```python
import jax
import jax.numpy as jnp
from jax import lax

HEADS = 10
HEAD_DIM = 64
C = 640
FRAMES = 8
TOKENS = 512


def draw_frames(key, part):
    shape = (FRAMES, TOKENS, HEADS * HEAD_DIM)
    base = jnp.clip(jax.random.normal(jax.random.fold_in(key, 14), shape, jnp.float32), -6.0, 6.0)
    return base.astype(jnp.bfloat16)


def draw_key_index(key, part):
    mixed_key = jax.random.fold_in(key, part)
    other = jax.random.randint(jax.random.fold_in(mixed_key, 21), (), 0, FRAMES - 1)
    last = jnp.array(FRAMES - 1, jnp.int32)
    coin = jax.random.randint(jax.random.fold_in(key, 22), (), 0, 2)
    flip = (coin + part) % 2
    first = jnp.where(flip == 1, last, other)
    second = jnp.where(flip == 1, other, last)
    return jnp.stack([first, second]).astype(jnp.int32)


def scatter_about(own_key, dims, scale, reach, held_as=jnp.bfloat16):
    return jnp.clip(scale * jax.random.normal(own_key, dims, jnp.float32), -reach, reach).astype(held_as)


def setup_inputs(seed: int = 0, part: int = 0) -> dict:
    arg_keys = jax.random.split(jax.random.key(seed), 9)
    own_keys = jax.random.split(jax.random.fold_in(arg_keys[8], part), 9)
    return {
        "frames": draw_frames(jax.random.fold_in(jax.random.fold_in(arg_keys[8], part), 71), part),
        "key_index": draw_key_index(jax.random.fold_in(jax.random.fold_in(arg_keys[8], part), 71), part),
        "w_query": scatter_about(arg_keys[2], (C, C), C ** -0.5, 0.25),
        "w_keyval": scatter_about(arg_keys[3], (C, 2 * C), C ** -0.5, 0.25),
        "w_out": scatter_about(arg_keys[4], (C, C), C ** -0.5, 0.25),
        "norm_gain": jnp.clip(1.0 + 0.18 * jax.random.normal(arg_keys[5], (C,), jnp.float32), 0.1, 1.9),
        "w_first": scatter_about(arg_keys[6], (3, C, C), (3 * C) ** -0.5, 0.125),
        "w_second": scatter_about(arg_keys[7], (3, C, C), (3 * C) ** -0.5, 0.125),
    }


def temporal_mix(padded, weights, count):
    result = jnp.zeros((count * padded.shape[1], padded.shape[2]), jnp.float32)
    for offset in range(3):
        window = padded[offset:offset + count].reshape(-1, padded.shape[2])
        result = result + jnp.dot(window, weights[offset], preferred_element_type=jnp.float32)
    return result

def reference(frames, key_index, w_query, w_keyval, w_out, norm_gain, w_first, w_second):
    channels = HEADS * HEAD_DIM
    scale = HEAD_DIM ** (-0.5)
    key_frames = frames[key_index.astype(jnp.int32)].reshape(-1, channels)
    keyval = jnp.dot(key_frames, w_keyval, preferred_element_type=jnp.float32).astype(jnp.bfloat16)
    key_heads = keyval[:, :channels].reshape(-1, HEADS, HEAD_DIM).astype(jnp.float32)
    value_heads = keyval[:, channels:].reshape(-1, HEADS, HEAD_DIM).astype(jnp.float32)

    def one_frame(tokens):
        queries = jnp.dot(tokens, w_query, preferred_element_type=jnp.float32).astype(jnp.bfloat16)
        query_heads = queries.reshape(-1, HEADS, HEAD_DIM).astype(jnp.float32)
        scores = jnp.einsum('qhd,khd->hqk', query_heads, key_heads) * scale
        highest = lax.optimization_barrier(jnp.max(scores, axis=-1, keepdims=True))
        exponent = jnp.exp(scores - highest)
        denominator = lax.optimization_barrier(jnp.sum(exponent, axis=-1))
        rounded = lax.optimization_barrier(exponent.astype(jnp.bfloat16))
        weights = rounded.astype(jnp.float32)
        mixed = jnp.einsum('hqk,khd->qhd', weights, value_heads) / denominator.T[:, :, None]
        attended = mixed.reshape(-1, channels).astype(jnp.bfloat16)
        residual = tokens.astype(jnp.float32) + jnp.dot(attended, w_out, preferred_element_type=jnp.float32)
        mean_square = lax.optimization_barrier(jnp.mean(residual * residual, axis=-1, keepdims=True))
        normed = (residual * lax.rsqrt(mean_square + 1e-06) * norm_gain.astype(jnp.float32)).astype(jnp.bfloat16)
        return (residual, normed)
    residual, normed = lax.map(one_frame, frames)
    frame_count = frames.shape[0]
    padded = jnp.pad(normed, ((1, 1), (0, 0), (0, 0)))
    first = temporal_mix(padded, w_first, frame_count)
    hidden = jax.nn.silu(first).astype(jnp.bfloat16).reshape(frame_count, -1, channels)
    padded = jnp.pad(hidden, ((1, 1), (0, 0), (0, 0)))
    second = temporal_mix(padded, w_second, frame_count)
    return (residual.reshape(-1, channels) + second).reshape(frames.shape).astype(jnp.bfloat16)
```

```python
import functools

import jax
import jax.numpy as jnp
from jax import lax
from jax.experimental import pallas as pl
from jax.experimental.pallas import tpu as pltpu
from jax.sharding import PartitionSpec as P

HEADS = 10
HEAD_DIM = 64
PAIR = 2 * HEAD_DIM
MESH = pl.DeviceIdType.MESH
F32 = jnp.float32
BF16 = jnp.bfloat16


def dot(a, b):
    return jnp.dot(a, b, preferred_element_type=F32)


def kernel(
    F, R,
    frames_ref, key_ref, gain_ref, wq_hbm, wkv_hbm, wo_hbm, w1_hbm, w2_hbm,
    out_ref,
    wq, wkv, wo, w1, w2, kbuf, cand, corebuf, xsrc, xdst,
    q_ref, kv_ref, m_ref, l_ref, acc_ref, att_ref, res_ref, nbuf, hbuf, conv_ref,
    wsem, asend, bsend, brecv, zsend, zrecv, csend, crecv, hsend, hrecv,
):
    T, _, H, C = frames_ref.shape
    N = 2 * H
    M = T * N
    me = lax.axis_index("frame")
    z = lax.axis_index("row")
    c = me % 2
    mate = me + 1 - 2 * c
    bits = F.bit_length() - 1

    loads = [
        pltpu.make_async_copy(src, dst, wsem.at[i])
        for i, (src, dst) in enumerate(
            [(wq_hbm, wq), (wkv_hbm, wkv), (wo_hbm, wo), (w1_hbm, w1), (w2_hbm, w2)]
        )
    ]
    for load in loads:
        load.start()

    barrier = pltpu.get_barrier_semaphore()
    for step in range(1, F):
        pl.semaphore_signal(barrier, 1, device_id={"frame": (me + step) % F}, device_id_type=MESH)
    for hop in (-2, -1, 1, 2):
        there = (z + hop >= 0) & (z + hop < R)

        @pl.when(there)
        def _():
            pl.semaphore_signal(barrier, 1, device_id={"row": z + hop}, device_id_type=MESH)

    other = key_ref[0] + key_ref[1] - (F * T - 1)
    owner = lax.div(other, T)
    local = lax.rem(other, T)
    chosen = frames_ref[0]
    for t in range(1, T):
        chosen = jnp.where(local == t, frames_ref[t], chosen)
    cand[...] = chosen

    @pl.when(me == F - 1)
    def _():
        kbuf[0, z, 1] = frames_ref[T - 1, 1]

    peers = F - 1
    for hop in (-2, -1, 1, 2):
        peers = peers + jnp.where((z + hop >= 0) & (z + hop < R), 1, 0)
    pl.semaphore_wait(barrier, peers)

    def remote(src, dst, ssem, rsem, **device):
        return pltpu.make_async_remote_copy(
            src_ref=src, dst_ref=dst, send_sem=ssem, recv_sem=rsem,
            device_id=device, device_id_type=MESH,
        )

    def last_copy(d):
        return remote(
            frames_ref.at[T - 1, d % 2], kbuf.at[0, z, d % 2],
            asend.at[d], zrecv.at[0, z], frame=d,
        )

    @pl.when(me == F - 1)
    def _():
        for d in range(F - 1):
            last_copy(d).start()

    core_swap = remote(cand.at[1 - c], corebuf, bsend.at[0], brecv.at[0], frame=mate)
    core_swap.start()

    def forward(key, way, d):
        o = z - way * d
        made = []
        for hop in (1, 2):
            dest = z + way * hop
            there = (o >= 0) & (o < R) & (dest >= 0) & (dest < R)
            copy = remote(
                kbuf.at[key, o, c], kbuf.at[key, o, c],
                zsend.at[key, (1 - way) // 2, d // 2, hop - 1], zrecv.at[key, o], row=dest,
            )
            made.append((there, copy))
        return made

    def core_copy(key, o):
        return remote(
            kbuf.at[key, o, c], kbuf.at[key, o, c], csend.at[key, o], crecv.at[key, o], frame=mate
        )

    def start_forward(key, way, d):
        for there, copy in forward(key, way, d):

            @pl.when(there)
            def _():
                copy.start()

    def launch_own(key):
        for way in (1, -1):
            start_forward(key, way, 0)
        core_copy(key, z).start()

    def service(key):
        for d in range(1, R):
            for way in (1, -1):
                o = z - way * d

                @pl.when((o >= 0) & (o < R))
                def _():
                    core_copy_z = remote(
                        kbuf.at[key, o, c], kbuf.at[key, o, c],
                        csend.at[key, o], zrecv.at[key, o], frame=mate,
                    )
                    core_copy_z.wait_recv()
                    if d % 2 == 0:
                        start_forward(key, way, d)
                    core_copy(key, o).start()

    loads[0].wait()
    q = dot(frames_ref[...].reshape(M, C), wq[...]).astype(BF16)
    q_ref[...] = q * BF16(HEAD_DIM ** -0.5)

    core_swap.wait_recv()
    current = jnp.where(lax.rem(owner, 2) == c, cand[c], corebuf[...])

    swaps = []
    for s in range(1, bits):
        bit = (me // 2 ** s) % 2
        partner = me + 2 ** s * (1 - 2 * bit)
        xsrc[s - 1] = current
        swap = remote(xsrc.at[s - 1], xdst.at[s - 1], bsend.at[s], brecv.at[s], frame=partner)
        swap.start()
        swaps.append(swap)
        if s == 1:

            @pl.when(me != F - 1)
            def _():
                remote(
                    frames_ref.at[T - 1, 0], kbuf.at[0, z, c],
                    asend.at[0], zrecv.at[0, z], frame=mate,
                ).wait_recv()

            launch_own(0)
        swap.wait_recv()
        current = jnp.where(lax.rem(lax.div(owner, 2 ** s), 2) == bit, current, xdst[s - 1])
    kbuf[1, z, c] = current
    launch_own(1)

    loads[1].wait()
    lane = lax.broadcasted_iota(jnp.int32, (1, PAIR), 1)
    keys = R * N
    ones = jnp.ones((keys, PAIR), BF16)

    def project(key):
        rows = kbuf[key].reshape(keys, C)

        def column(i, _):
            cols = pl.ds(pl.multiple_of(i * 256, 256), 256)
            kv_ref[:, cols] = dot(rows, wkv[:, cols]).astype(BF16)
            return 0

        lax.fori_loop(0, 2 * C // 256, column, 0)

    def attend(key):
        def pair(i, _):
            cols = pl.ds(pl.multiple_of(i * PAIR, PAIR), PAIR)
            vcols = pl.ds(pl.multiple_of(C + i * PAIR, PAIR), PAIR)
            qp = q_ref[:, cols]
            kp = kv_ref[:, cols]
            vp = jnp.concatenate([kv_ref[:, vcols], ones], axis=1)
            parts = []
            for side in range(2):
                mine = (lane < HEAD_DIM) if side == 0 else (lane >= HEAD_DIM)
                qh = jnp.where(mine, qp, BF16(0))
                scores = lax.dot_general(
                    qh, kp, (((1,), (1,)), ((), ())), preferred_element_type=F32
                )
                top = jnp.max(scores, axis=-1, keepdims=True)
                weights = jnp.exp(scores - top).astype(BF16)
                mixed = dot(weights, vp)
                parts.append((jnp.broadcast_to(top, (M, PAIR)), mixed[:, PAIR:], mixed[:, :PAIR]))
            top, low, acc = [jnp.where(lane < HEAD_DIM, a, b) for a, b in zip(*parts)]
            if key == 0:
                m_ref[:, cols] = top
                l_ref[:, cols] = low
                acc_ref[:, cols] = acc
            else:
                before = m_ref[:, cols]
                raised = jnp.maximum(before, top)
                old = jnp.exp(before - raised)
                new = jnp.exp(top - raised)
                total = acc_ref[:, cols] * old + acc * new
                att_ref[:, cols] = (total / (l_ref[:, cols] * old + low * new)).astype(BF16)
            return 0

        lax.fori_loop(0, HEADS // 2, pair, 0)

    for key in range(2):
        service(key)
        for o in range(R):
            core_copy(key, o).wait_recv()
        project(key)
        attend(key)

    loads[2].wait()
    res = frames_ref[...].reshape(M, C).astype(F32) + dot(att_ref[...], wo[...])
    res_ref[...] = res
    mean_square = jnp.mean(res * res, axis=-1, keepdims=True)
    normed = (res * lax.rsqrt(mean_square + 1e-06) * gain_ref[...]).astype(BF16)
    nbuf[N : N + M] = normed

    def halo(buf, stage):
        up = remote(
            buf.at[pl.ds(M, N)], buf.at[pl.ds(0, N)],
            hsend.at[stage, 0], hrecv.at[stage, 0], frame=(me + 1) % F,
        )
        down = remote(
            buf.at[pl.ds(N, N)], buf.at[pl.ds(N + M, N)],
            hsend.at[stage, 1], hrecv.at[stage, 1], frame=(me + F - 1) % F,
        )
        return up, down

    def start_halo(buf, stage):
        up, down = halo(buf, stage)

        @pl.when(me < F - 1)
        def _():
            up.start()

        @pl.when(me > 0)
        def _():
            down.start()

        @pl.when(me == 0)
        def _():
            buf[0:N] = jnp.zeros((N, C), BF16)

        @pl.when(me == F - 1)
        def _():
            buf[N + M : N + M + N] = jnp.zeros((N, C), BF16)

    def wait_halo(buf, stage):
        up, down = halo(buf, stage)

        @pl.when(me > 0)
        def _():
            up.wait_recv()

        @pl.when(me < F - 1)
        def _():
            down.wait_recv()

    def mix(buf, w, stage):
        inner = dot(buf[N : N + M], w[1])
        conv_ref[...] = inner
        conv_ref[N:M] += dot(buf[N:M], w[0])
        conv_ref[0 : M - N] += dot(buf[2 * N : N + M], w[2])
        wait_halo(buf, stage)
        conv_ref[0:N] += dot(buf[0:N], w[0])
        conv_ref[M - N : M] += dot(buf[N + M : N + M + N], w[2])
        return conv_ref[...]

    start_halo(nbuf, 0)
    loads[3].wait()
    first = mix(nbuf, w1, 0)
    hbuf[N : N + M] = (first / (1.0 + jnp.exp(-first))).astype(BF16)
    start_halo(hbuf, 1)
    loads[4].wait()
    second = mix(hbuf, w2, 1)
    out_ref[...] = (res_ref[...] + second).astype(BF16).reshape(out_ref.shape)

    @pl.when(me == F - 1)
    def _():
        for d in range(F - 1):
            last_copy(d).wait_send()

    core_swap.wait_send()
    for swap in swaps:
        swap.wait_send()
    for key in range(2):
        for o in range(R):
            core_copy(key, o).wait_send()
        for way in (1, -1):
            for d in range(0, R, 2):
                for there, copy in forward(key, way, d):

                    @pl.when(there)
                    def _():
                        copy.wait_send()

    for stage, buf in enumerate((nbuf, hbuf)):
        up, down = halo(buf, stage)

        @pl.when(me < F - 1)
        def _():
            up.wait_send()

        @pl.when(me > 0)
        def _():
            down.wait_send()


def shards(F, R, frames, key_index, w_query, w_keyval, w_out, norm_gain, w_first, w_second):
    T, N, C = frames.shape
    H, M, keys = N // 2, T * N, R * N
    bits = F.bit_length() - 1
    assert F == 2 ** bits and F >= 4
    vmem = pl.BlockSpec(memory_space=pltpu.VMEM)
    any_space = pl.BlockSpec(memory_space=pl.ANY)
    dma = pltpu.SemaphoreType.DMA
    out = pl.pallas_call(
        functools.partial(kernel, F, R),
        out_shape=jax.ShapeDtypeStruct((T, N, C), BF16),
        in_specs=[vmem, pl.BlockSpec(memory_space=pltpu.SMEM), vmem] + [any_space] * 5,
        out_specs=vmem,
        scratch_shapes=[
            pltpu.VMEM(w_query.shape, BF16),
            pltpu.VMEM(w_keyval.shape, BF16),
            pltpu.VMEM(w_out.shape, BF16),
            pltpu.VMEM(w_first.shape, BF16),
            pltpu.VMEM(w_second.shape, BF16),
            pltpu.VMEM((2, R, 2, H, C), BF16),
            pltpu.VMEM((2, H, C), BF16),
            pltpu.VMEM((H, C), BF16),
            pltpu.VMEM((bits - 1, H, C), BF16),
            pltpu.VMEM((bits - 1, H, C), BF16),
            pltpu.VMEM((M, C), BF16),
            pltpu.VMEM((keys, 2 * C), BF16),
            pltpu.VMEM((M, C), F32),
            pltpu.VMEM((M, C), F32),
            pltpu.VMEM((M, C), F32),
            pltpu.VMEM((M, C), BF16),
            pltpu.VMEM((M, C), F32),
            pltpu.VMEM((M + 2 * N, C), BF16),
            pltpu.VMEM((M + 2 * N, C), BF16),
            pltpu.VMEM((M, C), F32),
            dma((5,)),
            dma((F - 1,)),
            dma((bits,)),
            dma((bits,)),
            dma((2, 2, (R + 1) // 2, 2)),
            dma((2, R)),
            dma((2, R)),
            dma((2, R)),
            dma((2, 2)),
            dma((2, 2)),
        ],
        compiler_params=pltpu.CompilerParams(
            collective_id=0, has_side_effects=True, vmem_limit_bytes=48 * 2 ** 20
        ),
        cost_estimate=pl.CostEstimate(
            flops=5 * 10 ** 9, bytes_accessed=9 * 10 ** 6, transcendentals=M * keys * 2 * HEADS
        ),
    )(
        frames.reshape(T, 2, H, C), key_index, norm_gain.reshape(1, C),
        w_query, w_keyval, w_out, w_first, w_second,
    )
    return out


def solution(mesh):
    return jax.shard_map(
        functools.partial(shards, mesh.shape["frame"], mesh.shape["row"]),
        mesh=mesh,
        in_specs=(P(("clips", "frame"), "row", None), P("clips"), P(), P(), P(), P(), P(), P()),
        out_specs=P(("clips", "frame"), "row", None),
        check_vma=False,
    )
```

```python
import functools

import jax
import jax.numpy as jnp
from jax import lax
from jax.experimental import pallas as pl
from jax.experimental.pallas import tpu as pltpu
from jax.sharding import PartitionSpec as P

HEADS = 10
HEAD_DIM = 64
PAIR = 2 * HEAD_DIM
MESH = pl.DeviceIdType.MESH
F32 = jnp.float32
BF16 = jnp.bfloat16


def dot(a, b):
    return jnp.dot(a, b, preferred_element_type=F32)


def kernel(
    F, R,
    frames_ref, key_ref, gain_ref, wq_hbm, wkv_hbm, wo_hbm, w1_hbm, w2_hbm,
    out_ref,
    wq, wkv, wo, w1, w2, kbuf, cand, corebuf, xsrc, xdst,
    q_ref, kv_ref, m_ref, l_ref, acc_ref, att_ref, res_ref, nbuf, hbuf, conv_ref, sum_ref,
    wsem, asend, bsend, brecv, zsend, zrecv, xsend, xrecv, csend, crecv, hsend, hrecv,
):
    T, _, _, Q, C = frames_ref.shape
    N = 4 * Q
    M = T * N
    me = lax.axis_index("frame")
    z = lax.axis_index("row")
    c = me % 2
    x = (me // 2) % 2
    mate = me + 1 - 2 * c
    xmate = me + 2 - 4 * x
    bits = F.bit_length() - 1

    loads = [
        pltpu.make_async_copy(src, dst, wsem.at[i])
        for i, (src, dst) in enumerate(
            [(wq_hbm, wq), (wkv_hbm, wkv), (wo_hbm, wo), (w1_hbm, w1), (w2_hbm, w2)]
        )
    ]

    barrier = pltpu.get_barrier_semaphore()
    for step in range(1, F):
        pl.semaphore_signal(barrier, 1, device_id={"frame": (me + step) % F}, device_id_type=MESH)
    for step in range(1, R):
        pl.semaphore_signal(barrier, 1, device_id={"row": (z + step) % R}, device_id_type=MESH)
    for load in loads:
        load.start()

    other = key_ref[0] + key_ref[1] - (F * T - 1)
    owner = lax.div(other, T)
    local = lax.rem(other, T)
    chosen = frames_ref[0]
    for t in range(1, T):
        chosen = jnp.where(local == t, frames_ref[t], chosen)
    cand[...] = chosen

    @pl.when(me == F - 1)
    def _():
        kbuf[0, z, 1] = frames_ref[T - 1, 1]

    pl.semaphore_wait(barrier, F + R - 2)

    def remote(src, dst, ssem, rsem, **device):
        return pltpu.make_async_remote_copy(
            src_ref=src, dst_ref=dst, send_sem=ssem, recv_sem=rsem,
            device_id=device, device_id_type=MESH,
        )

    def last_copy(d):
        return remote(
            frames_ref.at[T - 1, d % 2], kbuf.at[0, z, d % 2],
            asend.at[d], zrecv.at[0, z], frame=d,
        )

    core_swap = remote(cand.at[1 - c], corebuf, bsend.at[0], brecv.at[0], frame=mate)
    core_swap.start()

    @pl.when(me == F - 1)
    def _():
        for d in range(F - 1):
            last_copy(d).start()

    def row_copy(key, way, d):
        dest = z + way * d
        block = kbuf.at[key, z, c] if d == 1 else kbuf.at[key, z, c, x]
        copy = remote(
            block, block, zsend.at[key, (1 - way) // 2, d - 1], zrecv.at[key, z], row=dest
        )
        return (dest >= 0) & (dest < R), copy

    def half_copy(key, o):
        block = kbuf.at[key, o, c]
        return remote(block, block, csend.at[key, o, 0], crecv.at[key, o, 0], frame=mate)

    def quarter_copy(key, o, which):
        block = kbuf.at[key, o, c, which]
        return remote(block, block, csend.at[key, o, which], crecv.at[key, o, which], frame=mate)

    def cross_copy(key, o):
        block = kbuf.at[key, o, c, x]
        return remote(block, block, xsend.at[key, o], xrecv.at[key, o], frame=xmate)

    def await_block(block, sem):
        remote(block, block, csend.at[0, 0, 0], sem, frame=mate).wait_recv()

    def launch_own(key):
        for d in range(1, R):
            for way in (1, -1):
                there, copy = row_copy(key, way, d)

                @pl.when(there)
                def _():
                    copy.start()

        half_copy(key, z).start()

    def origins(d):
        for way in (1, -1):
            o = z - way * d
            yield o, (o >= 0) & (o < R)

    def take_near(key):
        for o, there in origins(1):

            @pl.when(there)
            def _():
                await_block(kbuf.at[key, o, c], zrecv.at[key, o])
                half_copy(key, o).start()

    def take_far(key):
        for d in range(2, R):
            for o, there in origins(d):

                @pl.when(there)
                def _():
                    await_block(kbuf.at[key, o, c, x], zrecv.at[key, o])
                    cross_copy(key, o).start()
                    quarter_copy(key, o, x).start()

    def take_cross(key):
        for d in range(2, R):
            for o, there in origins(d):

                @pl.when(there)
                def _():
                    await_block(kbuf.at[key, o, c, 1 - x], xrecv.at[key, o])
                    quarter_copy(key, o, 1 - x).start()

    def await_near(key):
        await_block(kbuf.at[key, z, 1 - c], crecv.at[key, z, 0])
        for o, there in origins(1):

            @pl.when(there)
            def _():
                await_block(kbuf.at[key, o, 1 - c], crecv.at[key, o, 0])

    def await_far(key):
        for d in range(2, R):
            for o, there in origins(d):

                @pl.when(there)
                def _():
                    for which in range(2):
                        await_block(kbuf.at[key, o, 1 - c, which], crecv.at[key, o, which])

    loads[0].wait()
    q = dot(frames_ref[...].reshape(M, C), wq[...]).astype(BF16)
    q_ref[...] = q * BF16(HEAD_DIM ** -0.5)

    core_swap.wait_recv()
    current = jnp.where(lax.rem(owner, 2) == c, cand[c], corebuf[...])

    swaps = []
    for s in range(1, bits):
        bit = (me // 2 ** s) % 2
        partner = me + 2 ** s * (1 - 2 * bit)
        xsrc[s - 1] = current
        swap = remote(xsrc.at[s - 1], xdst.at[s - 1], bsend.at[s], brecv.at[s], frame=partner)
        swap.start()
        swaps.append(swap)
        if s == 1:

            @pl.when(me != F - 1)
            def _():
                await_block(kbuf.at[0, z, c], zrecv.at[0, z])

            launch_own(0)
        swap.wait_recv()
        current = jnp.where(lax.rem(lax.div(owner, 2 ** s), 2) == bit, current, xdst[s - 1])
    kbuf[1, z, c] = current
    launch_own(1)

    loads[1].wait()
    lane = lax.broadcasted_iota(jnp.int32, (1, PAIR), 1)
    reach = jnp.minimum(z, R - 1 - z)
    onward = jnp.where(z < R - 1 - z, 1, -1)
    per_chunk = 2
    ones = jnp.ones((per_chunk * N, PAIR), BF16)

    def nearest(j):
        d = jnp.where(j <= 2 * reach, (j + 1) // 2, j - reach)
        sign = jnp.where(j <= 2 * reach, 1 - 2 * (j % 2), onward)
        return z + sign * d

    def project(key, chunk):
        rows = jnp.concatenate(
            [kbuf[key, nearest(chunk * per_chunk + i)].reshape(N, C) for i in range(per_chunk)],
            axis=0,
        )
        kv_ref[...] = dot(rows, wkv[...]).astype(BF16)

    def attend(begin, end, rows, count):
        for i in range(HEADS // 2):
            cols = slice(i * PAIR, (i + 1) * PAIR)
            qp = q_ref[rows, cols]
            kp = kv_ref[:, cols]
            vp = jnp.concatenate([kv_ref[:, C + i * PAIR : C + (i + 1) * PAIR], ones], axis=1)
            parts = []
            for side in range(2):
                mine = (lane < HEAD_DIM) if side == 0 else (lane >= HEAD_DIM)
                qh = jnp.where(mine, qp, BF16(0))
                scores = lax.dot_general(
                    qh, kp, (((1,), (1,)), ((), ())), preferred_element_type=F32
                )
                top = jnp.max(scores, axis=-1, keepdims=True)
                weights = jnp.exp(scores - top).astype(BF16)
                mixed = dot(weights, vp)
                parts.append(
                    (jnp.broadcast_to(top, (count, PAIR)), mixed[:, PAIR:], mixed[:, :PAIR])
                )
            top, low, acc = [jnp.where(lane < HEAD_DIM, a, b) for a, b in zip(*parts)]
            if not begin:
                before = m_ref[rows, cols]
                raised = jnp.maximum(before, top)
                old = jnp.exp(before - raised)
                new = jnp.exp(top - raised)
                acc = acc_ref[rows, cols] * old + acc * new
                low = l_ref[rows, cols] * old + low * new
                top = raised
            if end:
                att_ref[rows, cols] = (acc / low).astype(BF16)
            else:
                m_ref[rows, cols] = top
                l_ref[rows, cols] = low
                acc_ref[rows, cols] = acc

    everything = slice(0, M)
    chunks = R // per_chunk
    take_near(0)
    await_near(0)
    project(0, 0)
    attend(True, False, everything, M)
    take_near(1)
    take_far(0)
    await_near(1)
    project(1, 0)
    attend(False, False, everything, M)
    take_cross(0)
    take_far(1)
    await_far(0)
    for chunk in range(1, chunks):
        project(0, chunk)
        attend(False, False, everything, M)
    take_cross(1)
    await_far(1)
    for chunk in range(1, chunks - 1):
        project(1, chunk)
        attend(False, False, everything, M)
    project(1, chunks - 1)

    def up_copy(f):
        k = f - (T - 2)
        return remote(
            nbuf.at[2 + f], nbuf.at[k], hsend.at[0, f], hrecv.at[0, k], frame=(me + 1) % F
        )

    def down_copy(f):
        return remote(
            nbuf.at[2 + f], nbuf.at[T + 2 + f], hsend.at[1, f], hrecv.at[1, f],
            frame=(me + F - 1) % F,
        )

    loads[2].wait()

    @pl.when(me == 0)
    def _():
        nbuf[0:2] = jnp.zeros((2, N, C), BF16)

    @pl.when(me == F - 1)
    def _():
        nbuf[T + 2 : T + 4] = jnp.zeros((2, N, C), BF16)

    for step in range(T):
        f = c * (T - 1 - step) + (1 - c) * step
        rows = pl.ds(pl.multiple_of(f * N, N), N)
        attend(False, True, rows, N)
        res = frames_ref[f].reshape(N, C).astype(F32) + dot(att_ref[rows, :], wo[...])
        res_ref[f] = res
        mean_square = jnp.mean(res * res, axis=-1, keepdims=True)
        gain = gain_ref[...].reshape(1, C)
        nbuf[2 + f] = (res * lax.rsqrt(mean_square + 1e-06) * gain).astype(BF16)

        @pl.when((me < F - 1) & (f >= T - 2))
        def _():
            up_copy(f).start()

        @pl.when((me > 0) & (f < 2))
        def _():
            down_copy(f).start()

    loads[3].wait()
    own = nbuf[2 : T + 2].reshape(M, C)
    for j in range(3):
        part = dot(own, w1[j]).reshape(T, N, C)
        if j == 0:
            conv_ref[0:2] = jnp.zeros((2, N, C), F32)
            conv_ref[2 : T + 2] = part
        else:
            conv_ref[2 - j : T + 2 - j] += part

    def exists(side):
        return ((side == 0) & (me > 0)) | ((side == 1) & (me < F - 1))

    sides = (1 - c, c)
    for side in sides:
        near = 1 + side * (T + 1)

        @pl.when(exists(side))
        def _():
            remote(
                nbuf.at[2], nbuf.at[near], hsend.at[0, 0], hrecv.at[side, 1 - side], frame=mate
            ).wait_recv()

        halo = nbuf[near]
        conv_ref[1 + side * (T - 1)] += dot(halo, w1[2 * side])
        conv_ref[side * (T + 1)] += dot(halo, w1[1])

    def silu(v):
        return v / (1.0 + jnp.exp(-v))

    hbuf[1 : T + 1] = silu(conv_ref[1 : T + 1]).astype(BF16)
    loads[4].wait()
    sum_ref[...] = res_ref[...] + dot(hbuf[1 : T + 1].reshape(M, C), w2[1]).reshape(T, N, C)
    inner = (T - 1) * N
    sum_ref[1:T] += dot(hbuf[1:T].reshape(inner, C), w2[0]).reshape(T - 1, N, C)
    sum_ref[0 : T - 1] += dot(hbuf[2 : T + 1].reshape(inner, C), w2[2]).reshape(T - 1, N, C)
    for side in sides:
        far = side * (T + 3)

        @pl.when(exists(side))
        def _():
            remote(
                nbuf.at[2], nbuf.at[far], hsend.at[0, 0], hrecv.at[side, side], frame=mate
            ).wait_recv()

        value = conv_ref[side * (T + 1)] + dot(nbuf[far], w1[2 * side])
        keep = jnp.where(exists(side), 1.0, 0.0)
        outer = (silu(value) * keep).astype(BF16)
        edge = side * (T - 1)
        sum_ref[edge] += dot(outer, w2[2 * side])
    out_ref[...] = sum_ref[...].astype(BF16)

    @pl.when(me == F - 1)
    def _():
        for d in range(F - 1):
            last_copy(d).wait_send()

    core_swap.wait_send()
    for swap in swaps:
        swap.wait_send()
    for key in range(2):
        half_copy(key, z).wait_send()
        for d in range(1, R):
            for way in (1, -1):
                reached, copy = row_copy(key, way, d)

                @pl.when(reached)
                def _():
                    copy.wait_send()

            for o, came in origins(d):

                @pl.when(came)
                def _():
                    if d == 1:
                        half_copy(key, o).wait_send()
                    else:
                        cross_copy(key, o).wait_send()
                        for which in range(2):
                            quarter_copy(key, o, which).wait_send()

    for f in range(T):

        @pl.when((me < F - 1) & (f >= T - 2))
        def _():
            up_copy(f).wait_send()

        @pl.when((me > 0) & (f < 2))
        def _():
            down_copy(f).wait_send()


def shards(F, R, frames, key_index, w_query, w_keyval, w_out, norm_gain, w_first, w_second):
    T, N, C = frames.shape
    Q, M = N // 4, T * N
    bits = F.bit_length() - 1
    assert F == 2 ** bits and F >= 4 and T >= 2 and R % 2 == 0 and R >= 4
    vmem = pl.BlockSpec(memory_space=pltpu.VMEM)
    any_space = pl.BlockSpec(memory_space=pl.ANY)
    dma = pltpu.SemaphoreType.DMA
    out = pl.pallas_call(
        functools.partial(kernel, F, R),
        out_shape=jax.ShapeDtypeStruct((T, N, C), BF16),
        in_specs=[vmem, pl.BlockSpec(memory_space=pltpu.SMEM), vmem] + [any_space] * 5,
        out_specs=vmem,
        scratch_shapes=[
            pltpu.VMEM(w_query.shape, BF16),
            pltpu.VMEM(w_keyval.shape, BF16),
            pltpu.VMEM(w_out.shape, BF16),
            pltpu.VMEM(w_first.shape, BF16),
            pltpu.VMEM(w_second.shape, BF16),
            pltpu.VMEM((2, R, 2, 2, Q, C), BF16),
            pltpu.VMEM((2, 2, Q, C), BF16),
            pltpu.VMEM((2, Q, C), BF16),
            pltpu.VMEM((bits - 1, 2, Q, C), BF16),
            pltpu.VMEM((bits - 1, 2, Q, C), BF16),
            pltpu.VMEM((M, C), BF16),
            pltpu.VMEM((2 * N, 2 * C), BF16),
            pltpu.VMEM((M, C), F32),
            pltpu.VMEM((M, C), F32),
            pltpu.VMEM((M, C), F32),
            pltpu.VMEM((M, C), BF16),
            pltpu.VMEM((T, N, C), F32),
            pltpu.VMEM((T + 4, N, C), BF16),
            pltpu.VMEM((T + 1, N, C), BF16),
            pltpu.VMEM((T + 2, N, C), F32),
            pltpu.VMEM((T, N, C), F32),
            dma((5,)),
            dma((F - 1,)),
            dma((bits,)),
            dma((bits,)),
            dma((2, 2, R - 1)),
            dma((2, R)),
            dma((2, R)),
            dma((2, R)),
            dma((2, R, 2)),
            dma((2, R, 2)),
            dma((2, T)),
            dma((2, 2)),
        ],
        compiler_params=pltpu.CompilerParams(
            collective_id=0, has_side_effects=True, vmem_limit_bytes=60 * 2 ** 20
        ),
        cost_estimate=pl.CostEstimate(
            flops=5 * 10 ** 9, bytes_accessed=9 * 10 ** 6,
            transcendentals=M * 2 * R * N * HEADS,
        ),
    )(
        frames.reshape(T, 2, 2, Q, C), key_index, norm_gain,
        w_query, w_keyval, w_out, w_first, w_second,
    )
    return out


def solution(mesh):
    return jax.shard_map(
        functools.partial(shards, mesh.shape["frame"], mesh.shape["row"]),
        mesh=mesh,
        in_specs=(P(("clips", "frame"), "row", None), P("clips"), P(), P(), P(), P(), P(), P()),
        out_specs=P(("clips", "frame"), "row", None),
        check_vma=False,
    )
```

```python
import functools

import jax
import jax.numpy as jnp
from jax import lax
from jax.experimental import pallas as pl
from jax.experimental.pallas import tpu as pltpu
from jax.sharding import PartitionSpec as P

HEADS = 10
HEAD_DIM = 64
PAIR = 2 * HEAD_DIM
MESH = pl.DeviceIdType.MESH
F32 = jnp.float32
BF16 = jnp.bfloat16


def dot(a, b):
    return jnp.dot(a, b, preferred_element_type=F32)


def kernel(
    F, R,
    frames_ref, key_ref, gain_ref, wq_hbm, wkv_hbm, wo_hbm, w1_hbm, w2_hbm,
    out_ref,
    wq, wkv, wo, w1, w2, kbuf, cand, corebuf, xsrc, xdst,
    q_ref, kv_ref, m_ref, l_ref, acc_ref, att_ref, res_ref, nbuf, hbuf, conv_ref,
    wsem, asend, bsend, brecv, zsend, zrecv, xsend, xrecv, csend, crecv, hsend, hrecv,
):
    T, _, _, Q, C = frames_ref.shape
    N = 4 * Q
    M = T * N
    me = lax.axis_index("frame")
    z = lax.axis_index("row")
    c = me % 2
    x = (me // 2) % 2
    mate = me + 1 - 2 * c
    xmate = me + 2 - 4 * x
    bits = F.bit_length() - 1

    loads = [
        pltpu.make_async_copy(src, dst, wsem.at[i])
        for i, (src, dst) in enumerate(
            [(wq_hbm, wq), (wkv_hbm, wkv), (wo_hbm, wo), (w1_hbm, w1), (w2_hbm, w2)]
        )
    ]

    barrier = pltpu.get_barrier_semaphore()
    for step in range(1, F):
        pl.semaphore_signal(barrier, 1, device_id={"frame": (me + step) % F}, device_id_type=MESH)
    for step in range(1, R):
        pl.semaphore_signal(barrier, 1, device_id={"row": (z + step) % R}, device_id_type=MESH)
    for load in loads:
        load.start()

    other = key_ref[0] + key_ref[1] - (F * T - 1)
    owner = lax.div(other, T)
    local = lax.rem(other, T)
    chosen = frames_ref[0]
    for t in range(1, T):
        chosen = jnp.where(local == t, frames_ref[t], chosen)
    cand[...] = chosen

    @pl.when(me == F - 1)
    def _():
        kbuf[0, z, 1] = frames_ref[T - 1, 1]

    pl.semaphore_wait(barrier, F + R - 2)

    def remote(src, dst, ssem, rsem, **device):
        return pltpu.make_async_remote_copy(
            src_ref=src, dst_ref=dst, send_sem=ssem, recv_sem=rsem,
            device_id=device, device_id_type=MESH,
        )

    def last_copy(d):
        return remote(
            frames_ref.at[T - 1, d % 2], kbuf.at[0, z, d % 2],
            asend.at[d], zrecv.at[0, z], frame=d,
        )

    core_swap = remote(cand.at[1 - c], corebuf, bsend.at[0], brecv.at[0], frame=mate)
    core_swap.start()

    @pl.when(me == F - 1)
    def _():
        for d in range(F - 1):
            last_copy(d).start()

    near = z + 1 - 2 * (z % 2)
    others = [
        2 * ((z // 2 + step) % (R // 2)) + i for step in range(1, R // 2) for i in range(2)
    ]

    def near_copy(key):
        block = kbuf.at[key, z, c]
        return remote(block, block, zsend.at[key, 0], zrecv.at[key, z], row=near)

    def far_copy(key, i):
        block = kbuf.at[key, z, c, x]
        return remote(block, block, zsend.at[key, 1 + i], zrecv.at[key, z], row=others[i])

    def half_copy(key, o):
        block = kbuf.at[key, o, c]
        return remote(block, block, csend.at[key, o, 0], crecv.at[key, o, 0], frame=mate)

    def quarter_copy(key, o, which):
        block = kbuf.at[key, o, c, which]
        return remote(block, block, csend.at[key, o, which], crecv.at[key, o, which], frame=mate)

    def cross_copy(key, o):
        block = kbuf.at[key, o, c, x]
        return remote(block, block, xsend.at[key, o], xrecv.at[key, o], frame=xmate)

    def await_block(block, sem):
        remote(block, block, csend.at[0, 0, 0], sem, frame=mate).wait_recv()

    def launch_own(key):
        near_copy(key).start()
        for i in range(R - 2):
            far_copy(key, i).start()
        half_copy(key, z).start()

    def take_near(key):
        await_block(kbuf.at[key, near, c], zrecv.at[key, near])
        half_copy(key, near).start()

    def take_far(key):
        for o in others:
            await_block(kbuf.at[key, o, c, x], zrecv.at[key, o])
            cross_copy(key, o).start()
            quarter_copy(key, o, x).start()

    def take_cross(key):
        for o in others:
            await_block(kbuf.at[key, o, c, 1 - x], xrecv.at[key, o])
            quarter_copy(key, o, 1 - x).start()

    def await_near(key):
        for o in (z, near):
            await_block(kbuf.at[key, o, 1 - c], crecv.at[key, o, 0])

    def await_far(key):
        for o in others:
            for which in range(2):
                await_block(kbuf.at[key, o, 1 - c, which], crecv.at[key, o, which])

    loads[0].wait()
    q = dot(frames_ref[...].reshape(M, C), wq[...]).astype(BF16)
    q_ref[...] = q * BF16(HEAD_DIM ** -0.5)

    core_swap.wait_recv()
    current = jnp.where(lax.rem(owner, 2) == c, cand[c], corebuf[...])

    swaps = []
    for s in range(1, bits):
        bit = (me // 2 ** s) % 2
        partner = me + 2 ** s * (1 - 2 * bit)
        xsrc[s - 1] = current
        swap = remote(xsrc.at[s - 1], xdst.at[s - 1], bsend.at[s], brecv.at[s], frame=partner)
        swap.start()
        swaps.append(swap)
        if s == 1:

            @pl.when(me != F - 1)
            def _():
                await_block(kbuf.at[0, z, c], zrecv.at[0, z])

            launch_own(0)
        swap.wait_recv()
        current = jnp.where(lax.rem(lax.div(owner, 2 ** s), 2) == bit, current, xdst[s - 1])
    kbuf[1, z, c] = current
    launch_own(1)

    loads[1].wait()
    lane = lax.broadcasted_iota(jnp.int32, (1, PAIR), 1)
    ones = jnp.ones((2 * N, PAIR), BF16)

    def project(key, chunk):
        pair = (z // 2 + chunk) % (R // 2)
        rows = kbuf[key, pl.ds(2 * pair, 2)].reshape(2 * N, C)
        kv_ref[...] = dot(rows, wkv[...]).astype(BF16)

    def attend(begin, end, rows, count):
        for i in range(HEADS // 2):
            cols = slice(i * PAIR, (i + 1) * PAIR)
            qp = q_ref[rows, cols]
            kp = kv_ref[:, cols]
            vp = jnp.concatenate([kv_ref[:, C + i * PAIR : C + (i + 1) * PAIR], ones], axis=1)
            parts = []
            for side in range(2):
                mine = (lane < HEAD_DIM) if side == 0 else (lane >= HEAD_DIM)
                qh = jnp.where(mine, qp, BF16(0))
                scores = lax.dot_general(
                    qh, kp, (((1,), (1,)), ((), ())), preferred_element_type=F32
                )
                top = jnp.max(scores, axis=-1, keepdims=True)
                weights = jnp.exp(scores - top).astype(BF16)
                mixed = dot(weights, vp)
                parts.append(
                    (jnp.broadcast_to(top, (count, PAIR)), mixed[:, PAIR:], mixed[:, :PAIR])
                )
            top, low, acc = [jnp.where(lane < HEAD_DIM, a, b) for a, b in zip(*parts)]
            if not begin:
                before = m_ref[rows, cols]
                raised = jnp.maximum(before, top)
                old = jnp.exp(before - raised)
                new = jnp.exp(top - raised)
                acc = acc_ref[rows, cols] * old + acc * new
                low = l_ref[rows, cols] * old + low * new
                top = raised
            if end:
                att_ref[rows, cols] = (acc / low).astype(BF16)
            else:
                m_ref[rows, cols] = top
                l_ref[rows, cols] = low
                acc_ref[rows, cols] = acc

    everything = slice(0, M)
    chunks = R // 2
    take_near(0)
    await_near(0)
    project(0, 0)
    attend(True, False, everything, M)
    take_near(1)
    take_far(0)
    await_near(1)
    project(1, 0)
    attend(False, False, everything, M)
    take_cross(0)
    take_far(1)
    await_far(0)
    for chunk in range(1, chunks):
        project(0, chunk)
        attend(False, False, everything, M)
    take_cross(1)
    await_far(1)
    for chunk in range(1, chunks - 1):
        project(1, chunk)
        attend(False, False, everything, M)
    project(1, chunks - 1)

    def up_copy(f, piece):
        k, rows = f - (T - 2), pl.ds(piece * N // 2, N // 2)
        return remote(
            nbuf.at[2 + f, rows], nbuf.at[k, rows],
            hsend.at[0, f, piece], hrecv.at[0, k, piece], frame=(me + 1) % F,
        )

    def down_copy(f, piece):
        rows = pl.ds(piece * N // 2, N // 2)
        return remote(
            nbuf.at[2 + f, rows], nbuf.at[T + 2 + f, rows],
            hsend.at[1, f, piece], hrecv.at[1, f, piece], frame=(me + F - 1) % F,
        )

    def await_halo(side, slot, k):
        for piece in range(2):
            await_block(nbuf.at[slot, pl.ds(piece * N // 2, N // 2)], hrecv.at[side, k, piece])

    loads[2].wait()

    @pl.when(me == 0)
    def _():
        nbuf[0:2] = jnp.zeros((2, N, C), BF16)

    @pl.when(me == F - 1)
    def _():
        nbuf[T + 2 : T + 4] = jnp.zeros((2, N, C), BF16)

    for step in range(T):
        f = c * (T - 1 - step) + (1 - c) * step
        rows = pl.ds(pl.multiple_of(f * N, N), N)
        attend(False, True, rows, N)
        res = frames_ref[f].reshape(N, C).astype(F32) + dot(att_ref[rows, :], wo[...])
        res_ref[f] = res
        mean_square = jnp.mean(res * res, axis=-1, keepdims=True)
        gain = gain_ref[...].reshape(1, C)
        nbuf[2 + f] = (res * lax.rsqrt(mean_square + 1e-06) * gain).astype(BF16)

        @pl.when((me < F - 1) & (f >= T - 2))
        def _():
            for piece in range(2):
                up_copy(f, piece).start()

        @pl.when((me > 0) & (f < 2))
        def _():
            for piece in range(2):
                down_copy(f, piece).start()

    loads[3].wait()
    own = nbuf[2 : T + 2].reshape(M, C)
    for j in range(3):
        part = dot(own, w1[j]).reshape(T, N, C)
        if j == 0:
            conv_ref[0:2] = jnp.zeros((2, N, C), F32)
            conv_ref[2 : T + 2] = part
        else:
            conv_ref[2 - j : T + 2 - j] += part

    def exists(side):
        return ((side == 0) & (me > 0)) | ((side == 1) & (me < F - 1))

    sides = (1 - c, c)
    for side in sides:
        beside = 1 + side * (T + 1)

        @pl.when(exists(side))
        def _():
            await_halo(side, beside, 1 - side)

        halo = nbuf[beside]
        conv_ref[1 + side * (T - 1)] += dot(halo, w1[2 * side])
        conv_ref[side * (T + 1)] += dot(halo, w1[1])

    def silu(v):
        return v / (1.0 + jnp.exp(-v))

    hbuf[1 : T + 1] = silu(conv_ref[1 : T + 1]).astype(BF16)
    loads[4].wait()
    out_ref[...] = res_ref[...] + dot(hbuf[1 : T + 1].reshape(M, C), w2[1]).reshape(T, N, C)
    inner = (T - 1) * N
    out_ref[1:T] += dot(hbuf[1:T].reshape(inner, C), w2[0]).reshape(T - 1, N, C)
    out_ref[0 : T - 1] += dot(hbuf[2 : T + 1].reshape(inner, C), w2[2]).reshape(T - 1, N, C)
    for side in sides:
        far = side * (T + 3)

        @pl.when(exists(side))
        def _():
            await_halo(side, far, side)

        value = conv_ref[side * (T + 1)] + dot(nbuf[far], w1[2 * side])
        keep = jnp.where(exists(side), 1.0, 0.0)
        outer = (silu(value) * keep).astype(BF16)
        edge = side * (T - 1)
        out_ref[edge] += dot(outer, w2[2 * side])

    @pl.when(me == F - 1)
    def _():
        for d in range(F - 1):
            last_copy(d).wait_send()

    core_swap.wait_send()
    for swap in swaps:
        swap.wait_send()
    for key in range(2):
        near_copy(key).wait_send()
        half_copy(key, z).wait_send()
        half_copy(key, near).wait_send()
        for i, o in enumerate(others):
            far_copy(key, i).wait_send()
            cross_copy(key, o).wait_send()
            for which in range(2):
                quarter_copy(key, o, which).wait_send()

    for f in range(T):

        @pl.when((me < F - 1) & (f >= T - 2))
        def _():
            for piece in range(2):
                up_copy(f, piece).wait_send()

        @pl.when((me > 0) & (f < 2))
        def _():
            for piece in range(2):
                down_copy(f, piece).wait_send()


def shards(F, R, frames, key_index, w_query, w_keyval, w_out, norm_gain, w_first, w_second):
    T, N, C = frames.shape
    Q, M = N // 4, T * N
    bits = F.bit_length() - 1
    assert F == 2 ** bits and F >= 4 and T >= 2 and R % 2 == 0 and R >= 4
    vmem = pl.BlockSpec(memory_space=pltpu.VMEM)
    any_space = pl.BlockSpec(memory_space=pl.ANY)
    dma = pltpu.SemaphoreType.DMA
    out = pl.pallas_call(
        functools.partial(kernel, F, R),
        out_shape=jax.ShapeDtypeStruct((T, N, C), F32),
        in_specs=[vmem, pl.BlockSpec(memory_space=pltpu.SMEM), vmem] + [any_space] * 5,
        out_specs=vmem,
        scratch_shapes=[
            pltpu.VMEM(w_query.shape, BF16),
            pltpu.VMEM(w_keyval.shape, BF16),
            pltpu.VMEM(w_out.shape, BF16),
            pltpu.VMEM(w_first.shape, BF16),
            pltpu.VMEM(w_second.shape, BF16),
            pltpu.VMEM((2, R, 2, 2, Q, C), BF16),
            pltpu.VMEM((2, 2, Q, C), BF16),
            pltpu.VMEM((2, Q, C), BF16),
            pltpu.VMEM((bits - 1, 2, Q, C), BF16),
            pltpu.VMEM((bits - 1, 2, Q, C), BF16),
            pltpu.VMEM((M, C), BF16),
            pltpu.VMEM((2 * N, 2 * C), BF16),
            pltpu.VMEM((M, C), F32),
            pltpu.VMEM((M, C), F32),
            pltpu.VMEM((M, C), F32),
            pltpu.VMEM((M, C), BF16),
            pltpu.VMEM((T, N, C), F32),
            pltpu.VMEM((T + 4, N, C), BF16),
            pltpu.VMEM((T + 1, N, C), BF16),
            pltpu.VMEM((T + 2, N, C), F32),
            dma((5,)),
            dma((F - 1,)),
            dma((bits,)),
            dma((bits,)),
            dma((2, R - 1)),
            dma((2, R)),
            dma((2, R)),
            dma((2, R)),
            dma((2, R, 2)),
            dma((2, R, 2)),
            dma((2, T, 2)),
            dma((2, 2, 2)),
        ],
        compiler_params=pltpu.CompilerParams(
            collective_id=0, has_side_effects=True, vmem_limit_bytes=60 * 2 ** 20
        ),
        cost_estimate=pl.CostEstimate(
            flops=5 * 10 ** 9, bytes_accessed=9 * 10 ** 6,
            transcendentals=M * 2 * R * N * HEADS,
        ),
    )(
        frames.reshape(T, 2, 2, Q, C), key_index, norm_gain,
        w_query, w_keyval, w_out, w_first, w_second,
    )
    return out.astype(BF16)


def solution(mesh):
    return jax.shard_map(
        functools.partial(shards, mesh.shape["frame"], mesh.shape["row"]),
        mesh=mesh,
        in_specs=(P(("clips", "frame"), "row", None), P("clips"), P(), P(), P(), P(), P(), P()),
        out_specs=P(("clips", "frame"), "row", None),
        check_vma=False,
    )
```

```python
import functools

import jax
import jax.numpy as jnp
from jax import lax
from jax.experimental import pallas as pl
from jax.experimental.pallas import tpu as pltpu
from jax.sharding import PartitionSpec as P

HEADS = 10
HEAD_DIM = 64
PAIR = 2 * HEAD_DIM
MESH = pl.DeviceIdType.MESH
F32 = jnp.float32
BF16 = jnp.bfloat16


def dot(a, b):
    return jnp.dot(a, b, preferred_element_type=F32)


def kernel(
    F, R,
    frames_ref, key_ref, gain_ref, wq_hbm, wkv_hbm, wo_hbm, w1_hbm, w2_hbm,
    out_ref,
    wq, wkv, wo, w1, w2, kbuf, cand, corebuf, xsrc, xdst, raw,
    q_ref, kv_ref, m_ref, l_ref, acc_ref, att_ref, res_ref, nbuf, hbuf,
    wsem, asend, bsend, brecv, zsend, zrecv, xsend, xrecv, csend, crecv, hsend, hrecv,
):
    T, _, _, Q, C = frames_ref.shape
    N = 4 * Q
    M = T * N
    me = lax.axis_index("frame")
    z = lax.axis_index("row")
    c = me % 2
    x = (me // 2) % 2
    mate = me + 1 - 2 * c
    xmate = me + 2 - 4 * x
    bits = F.bit_length() - 1
    outer = me + 2 * c - 1
    has_outer = (outer >= 0) & (outer < F)

    loads = [
        pltpu.make_async_copy(src, dst, wsem.at[i])
        for i, (src, dst) in enumerate(
            [(wq_hbm, wq), (wkv_hbm, wkv), (wo_hbm, wo), (w1_hbm, w1), (w2_hbm, w2)]
        )
    ]

    barrier = pltpu.get_barrier_semaphore()
    for step in range(1, F):
        pl.semaphore_signal(barrier, 1, device_id={"frame": (me + step) % F}, device_id_type=MESH)
    for step in range(1, R):
        pl.semaphore_signal(barrier, 1, device_id={"row": (z + step) % R}, device_id_type=MESH)
    for load in loads:
        load.start()

    other = key_ref[0] + key_ref[1] - (F * T - 1)
    owner = lax.div(other, T)
    local = lax.rem(other, T)
    chosen = frames_ref[0]
    for t in range(1, T):
        chosen = jnp.where(local == t, frames_ref[t], chosen)
    cand[...] = chosen

    @pl.when(me == F - 1)
    def _():
        kbuf[0, z, 1] = frames_ref[T - 1, 1]

    @pl.when((outer < 0) | (outer >= F))
    def _():
        raw[...] = jnp.zeros_like(raw)

    pl.semaphore_wait(barrier, F + R - 2)

    def remote(src, dst, ssem, rsem, **device):
        return pltpu.make_async_remote_copy(
            src_ref=src, dst_ref=dst, send_sem=ssem, recv_sem=rsem,
            device_id=device, device_id_type=MESH,
        )

    def last_copy(d):
        return remote(
            frames_ref.at[T - 1, d % 2], kbuf.at[0, z, d % 2],
            asend.at[d], zrecv.at[0, z], frame=d,
        )

    raw_copy = remote(
        frames_ref.at[pl.ds(c * (T - 2), 2)], raw, hsend.at[0], hrecv.at[0], frame=outer
    )
    inner_copy = remote(
        nbuf.at[pl.ds(2 + (1 - c) * (T - 2), 2)], nbuf.at[pl.ds(c * (T + 2), 2)],
        hsend.at[1], hrecv.at[1], frame=mate,
    )

    core_swap = remote(cand.at[1 - c], corebuf, bsend.at[0], brecv.at[0], frame=mate)
    core_swap.start()

    @pl.when(me == F - 1)
    def _():
        for d in range(F - 1):
            last_copy(d).start()

    near = z + 1 - 2 * (z % 2)
    others = [
        2 * ((z // 2 + step) % (R // 2)) + i for step in range(1, R // 2) for i in range(2)
    ]

    def near_copy(key):
        block = kbuf.at[key, z, c]
        return remote(block, block, zsend.at[key, 0], zrecv.at[key, z], row=near)

    def far_copy(key, i):
        block = kbuf.at[key, z, c, x]
        return remote(block, block, zsend.at[key, 1 + i], zrecv.at[key, z], row=others[i])

    def half_copy(key, o):
        block = kbuf.at[key, o, c]
        return remote(block, block, csend.at[key, o, 0], crecv.at[key, o, 0], frame=mate)

    def quarter_copy(key, o, which):
        block = kbuf.at[key, o, c, which]
        return remote(block, block, csend.at[key, o, which], crecv.at[key, o, which], frame=mate)

    def cross_copy(key, o):
        block = kbuf.at[key, o, c, x]
        return remote(block, block, xsend.at[key, o], xrecv.at[key, o], frame=xmate)

    def await_block(block, sem):
        remote(block, block, csend.at[0, 0, 0], sem, frame=mate).wait_recv()

    def launch_own(key):
        near_copy(key).start()
        for i in range(R - 2):
            far_copy(key, i).start()
        half_copy(key, z).start()

    def take_near(key):
        await_block(kbuf.at[key, near, c], zrecv.at[key, near])
        half_copy(key, near).start()

    def take_far(key):
        for o in others:
            await_block(kbuf.at[key, o, c, x], zrecv.at[key, o])
            cross_copy(key, o).start()
            quarter_copy(key, o, x).start()

    def take_cross(key):
        for o in others:
            await_block(kbuf.at[key, o, c, 1 - x], xrecv.at[key, o])
            quarter_copy(key, o, 1 - x).start()

    def await_near(key):
        for o in (z, near):
            await_block(kbuf.at[key, o, 1 - c], crecv.at[key, o, 0])

    def await_far(key):
        for o in others:
            for which in range(2):
                await_block(kbuf.at[key, o, 1 - c, which], crecv.at[key, o, which])

    loads[0].wait()
    q = dot(frames_ref[...].reshape(M, C), wq[...]).astype(BF16)
    q_ref[0:M] = q * BF16(HEAD_DIM ** -0.5)

    core_swap.wait_recv()
    current = jnp.where(lax.rem(owner, 2) == c, cand[c], corebuf[...])

    swaps = []
    for s in range(1, bits):
        bit = (me // 2 ** s) % 2
        partner = me + 2 ** s * (1 - 2 * bit)
        xsrc[s - 1] = current
        swap = remote(xsrc.at[s - 1], xdst.at[s - 1], bsend.at[s], brecv.at[s], frame=partner)
        swap.start()
        swaps.append(swap)
        if s == 1:

            @pl.when(me != F - 1)
            def _():
                await_block(kbuf.at[0, z, c], zrecv.at[0, z])

            launch_own(0)

            @pl.when(has_outer)
            def _():
                raw_copy.start()

        swap.wait_recv()
        current = jnp.where(lax.rem(lax.div(owner, 2 ** s), 2) == bit, current, xdst[s - 1])
    kbuf[1, z, c] = current
    launch_own(1)

    loads[1].wait()
    lane = lax.broadcasted_iota(jnp.int32, (1, PAIR), 1)
    ones = jnp.ones((2 * N, PAIR), BF16)

    def project(key, chunk):
        pair = (z // 2 + chunk) % (R // 2)
        rows = kbuf[key, pl.ds(2 * pair, 2)].reshape(2 * N, C)
        kv_ref[...] = dot(rows, wkv[...]).astype(BF16)

    def attend(begin, end, rows, count):
        for i in range(HEADS // 2):
            cols = slice(i * PAIR, (i + 1) * PAIR)
            qp = q_ref[rows, cols]
            kp = kv_ref[:, cols]
            vp = jnp.concatenate([kv_ref[:, C + i * PAIR : C + (i + 1) * PAIR], ones], axis=1)
            parts = []
            for side in range(2):
                mine = (lane < HEAD_DIM) if side == 0 else (lane >= HEAD_DIM)
                qh = jnp.where(mine, qp, BF16(0))
                scores = lax.dot_general(
                    qh, kp, (((1,), (1,)), ((), ())), preferred_element_type=F32
                )
                top = jnp.max(scores, axis=-1, keepdims=True)
                weights = jnp.exp(scores - top).astype(BF16)
                mixed = dot(weights, vp)
                parts.append(
                    (jnp.broadcast_to(top, (count, PAIR)), mixed[:, PAIR:], mixed[:, :PAIR])
                )
            top, low, acc = [jnp.where(lane < HEAD_DIM, a, b) for a, b in zip(*parts)]
            if not begin:
                before = m_ref[rows, cols]
                raised = jnp.maximum(before, top)
                old = jnp.exp(before - raised)
                new = jnp.exp(top - raised)
                acc = acc_ref[rows, cols] * old + acc * new
                low = l_ref[rows, cols] * old + low * new
                top = raised
            if end:
                att_ref[rows, cols] = (acc / low).astype(BF16)
            else:
                m_ref[rows, cols] = top
                l_ref[rows, cols] = low
                acc_ref[rows, cols] = acc

    halves = (slice(0, M), slice(M, M + 2 * N))

    def chunk(key, index, begin=False):
        project(key, index)
        for rows in halves:
            attend(begin, False, rows, rows.stop - rows.start)

    chunks = R // 2
    take_near(0)
    await_near(0)
    project(0, 0)
    attend(True, False, halves[0], M)

    @pl.when(has_outer)
    def _():
        raw_copy.wait_recv()

    q = dot(raw[...].reshape(2 * N, C), wq[...]).astype(BF16)
    q_ref[M : M + 2 * N] = q * BF16(HEAD_DIM ** -0.5)
    take_far(0)
    take_near(1)
    attend(True, False, halves[1], 2 * N)
    await_near(1)
    chunk(1, 0)
    take_cross(0)
    take_far(1)
    await_far(0)
    for index in range(1, chunks):
        chunk(0, index)
    take_cross(1)
    await_far(1)
    for index in range(1, chunks - 1):
        chunk(1, index)
    project(1, chunks - 1)
    loads[2].wait()

    def finish(rows, tokens):
        count = rows.stop - rows.start
        attend(False, True, rows, count)
        res = tokens.reshape(count, C).astype(F32) + dot(att_ref[rows, :], wo[...])
        mean_square = jnp.mean(res * res, axis=-1, keepdims=True)
        gain = gain_ref[...].reshape(1, C)
        normed = (res * lax.rsqrt(mean_square + 1e-06) * gain).astype(BF16)
        return res.reshape(count // N, N, C), normed.reshape(count // N, N, C)

    res, normed = finish(halves[0], frames_ref[...])
    res_ref[...] = res
    nbuf[2 : T + 2] = normed
    inner_copy.start()
    _, normed = finish(halves[1], raw[...])
    nbuf[pl.ds(c * (T + 2), 2)] = jnp.where(has_outer, normed, jnp.zeros_like(normed))

    loads[3].wait()
    loads[4].wait()
    await_block(nbuf.at[pl.ds((1 - c) * (T + 2), 2)], hrecv.at[1])
    first = sum(dot(nbuf[j : j + T + 2].reshape(M + 2 * N, C), w1[j]) for j in range(3))
    hidden = first / (1.0 + jnp.exp(-first))
    hbuf[...] = hidden.astype(BF16).reshape(T + 2, N, C)

    @pl.when(me == 0)
    def _():
        hbuf[0] = jnp.zeros((N, C), BF16)

    @pl.when(me == F - 1)
    def _():
        hbuf[T + 1] = jnp.zeros((N, C), BF16)

    second = sum(dot(hbuf[j : j + T].reshape(M, C), w2[j]) for j in range(3))
    out_ref[...] = (res_ref[...] + second.reshape(T, N, C)).astype(BF16)

    @pl.when(me == F - 1)
    def _():
        for d in range(F - 1):
            last_copy(d).wait_send()

    core_swap.wait_send()
    for swap in swaps:
        swap.wait_send()
    for key in range(2):
        near_copy(key).wait_send()
        half_copy(key, z).wait_send()
        half_copy(key, near).wait_send()
        for i, o in enumerate(others):
            far_copy(key, i).wait_send()
            cross_copy(key, o).wait_send()
            for which in range(2):
                quarter_copy(key, o, which).wait_send()

    inner_copy.wait_send()

    @pl.when(has_outer)
    def _():
        raw_copy.wait_send()


def shards(F, R, frames, key_index, w_query, w_keyval, w_out, norm_gain, w_first, w_second):
    T, N, C = frames.shape
    Q, M = N // 4, T * N
    bits = F.bit_length() - 1
    assert F == 2 ** bits and F >= 4 and T >= 2 and R % 2 == 0 and R >= 4
    vmem = pl.BlockSpec(memory_space=pltpu.VMEM)
    hbm = pl.BlockSpec(memory_space=pltpu.HBM)
    dma = pltpu.SemaphoreType.DMA
    out = pl.pallas_call(
        functools.partial(kernel, F, R),
        out_shape=jax.ShapeDtypeStruct((T, N, C), BF16),
        in_specs=[vmem, pl.BlockSpec(memory_space=pltpu.SMEM), vmem] + [hbm] * 5,
        out_specs=vmem,
        scratch_shapes=[
            pltpu.VMEM(w_query.shape, BF16),
            pltpu.VMEM(w_keyval.shape, BF16),
            pltpu.VMEM(w_out.shape, BF16),
            pltpu.VMEM(w_first.shape, BF16),
            pltpu.VMEM(w_second.shape, BF16),
            pltpu.VMEM((2, R, 2, 2, Q, C), BF16),
            pltpu.VMEM((2, 2, Q, C), BF16),
            pltpu.VMEM((2, Q, C), BF16),
            pltpu.VMEM((bits - 1, 2, Q, C), BF16),
            pltpu.VMEM((bits - 1, 2, Q, C), BF16),
            pltpu.VMEM((2, 2, 2, Q, C), BF16),
            pltpu.VMEM((M + 2 * N, C), BF16),
            pltpu.VMEM((2 * N, 2 * C), BF16),
            pltpu.VMEM((M + 2 * N, C), F32),
            pltpu.VMEM((M + 2 * N, C), F32),
            pltpu.VMEM((M + 2 * N, C), F32),
            pltpu.VMEM((M + 2 * N, C), BF16),
            pltpu.VMEM((T, N, C), F32),
            pltpu.VMEM((T + 4, N, C), BF16),
            pltpu.VMEM((T + 2, N, C), BF16),
            dma((5,)),
            dma((F - 1,)),
            dma((bits,)),
            dma((bits,)),
            dma((2, R - 1)),
            dma((2, R)),
            dma((2, R)),
            dma((2, R)),
            dma((2, R, 2)),
            dma((2, R, 2)),
            dma((2,)),
            dma((2,)),
        ],
        compiler_params=pltpu.CompilerParams(
            collective_id=0, has_side_effects=True, vmem_limit_bytes=60 * 2 ** 20
        ),
        cost_estimate=pl.CostEstimate(
            flops=5 * 10 ** 9, bytes_accessed=9 * 10 ** 6,
            transcendentals=M * 2 * R * N * HEADS,
        ),
    )(
        frames.reshape(T, 2, 2, Q, C), key_index, norm_gain,
        w_query, w_keyval, w_out, w_first, w_second,
    )
    return out


def solution(mesh):
    return jax.shard_map(
        functools.partial(shards, mesh.shape["frame"], mesh.shape["row"]),
        mesh=mesh,
        in_specs=(P(("clips", "frame"), "row", None), P("clips"), P(), P(), P(), P(), P(), P()),
        out_specs=P(("clips", "frame"), "row", None),
        check_vma=False,
    )
```

```python
import functools

import jax
import jax.numpy as jnp
from jax import lax
from jax.experimental import pallas as pl
from jax.experimental.pallas import tpu as pltpu
from jax.sharding import PartitionSpec as P

HEADS = 10
HEAD_DIM = 64
PAIR = 2 * HEAD_DIM
MESH = pl.DeviceIdType.MESH
F32 = jnp.float32
BF16 = jnp.bfloat16


def dot(a, b):
    return jnp.dot(a, b, preferred_element_type=F32)


def kernel(
    F, R,
    frames_ref, key_ref, gain_ref, wq_hbm, wkv_hbm, wo_hbm, w1_hbm, w2_hbm,
    out_ref,
    wq, wkv, wo, w1, w2, kbuf, cand, corebuf, xsrc, xdst, raw,
    wvt, q_ref, k_ref, v_ref, m_ref, l_ref, acc_ref, att_ref, res_ref, nbuf, hbuf,
    wsem, asend, bsend, brecv, zsend, zrecv, xsend, xrecv, csend, crecv, hsend, hrecv,
):
    T, _, _, Q, C = frames_ref.shape
    N = 4 * Q
    M = T * N
    me = lax.axis_index("frame")
    z = lax.axis_index("row")
    c = me % 2
    x = (me // 2) % 2
    mate = me + 1 - 2 * c
    xmate = me + 2 - 4 * x
    bits = F.bit_length() - 1
    outer = me + 2 * c - 1
    has_outer = (outer >= 0) & (outer < F)

    loads = [
        pltpu.make_async_copy(src, dst, wsem.at[i])
        for i, (src, dst) in enumerate(
            [(wq_hbm, wq), (wkv_hbm, wkv), (wo_hbm, wo), (w1_hbm, w1), (w2_hbm, w2)]
        )
    ]

    barrier = pltpu.get_barrier_semaphore()
    for step in range(1, F):
        pl.semaphore_signal(barrier, 1, device_id={"frame": (me + step) % F}, device_id_type=MESH)
    for step in range(1, R):
        pl.semaphore_signal(barrier, 1, device_id={"row": (z + step) % R}, device_id_type=MESH)
    for load in loads:
        load.start()

    other = key_ref[0] + key_ref[1] - (F * T - 1)
    owner = lax.div(other, T)
    local = lax.rem(other, T)
    chosen = frames_ref[0]
    for t in range(1, T):
        chosen = jnp.where(local == t, frames_ref[t], chosen)
    cand[...] = chosen

    @pl.when(me == F - 1)
    def _():
        kbuf[0, z, 1] = frames_ref[T - 1, 1]

    @pl.when((outer < 0) | (outer >= F))
    def _():
        raw[...] = jnp.zeros_like(raw)

    pl.semaphore_wait(barrier, F + R - 2)

    def remote(src, dst, ssem, rsem, **device):
        return pltpu.make_async_remote_copy(
            src_ref=src, dst_ref=dst, send_sem=ssem, recv_sem=rsem,
            device_id=device, device_id_type=MESH,
        )

    def last_copy(d):
        return remote(
            frames_ref.at[T - 1, d % 2], kbuf.at[0, z, d % 2],
            asend.at[d], zrecv.at[0, z], frame=d,
        )

    raw_copy = remote(
        frames_ref.at[pl.ds(c * (T - 2), 2)], raw, hsend.at[0], hrecv.at[0], frame=outer
    )
    inner_copy = remote(
        nbuf.at[pl.ds(2 + (1 - c) * (T - 2), 2)], nbuf.at[pl.ds(c * (T + 2), 2)],
        hsend.at[1], hrecv.at[1], frame=mate,
    )

    core_swap = remote(cand.at[1 - c], corebuf, bsend.at[0], brecv.at[0], frame=mate)
    core_swap.start()

    @pl.when(me == F - 1)
    def _():
        for d in range(F - 1):
            last_copy(d).start()

    near = z + 1 - 2 * (z % 2)
    others = [
        2 * ((z // 2 + step) % (R // 2)) + i for step in range(1, R // 2) for i in range(2)
    ]

    def near_copy(key):
        block = kbuf.at[key, z, c]
        return remote(block, block, zsend.at[key, 0], zrecv.at[key, z], row=near)

    def far_copy(key, i):
        block = kbuf.at[key, z, c, x]
        return remote(block, block, zsend.at[key, 1 + i], zrecv.at[key, z], row=others[i])

    def half_copy(key, o):
        block = kbuf.at[key, o, c]
        return remote(block, block, csend.at[key, o, 0], crecv.at[key, o, 0], frame=mate)

    def quarter_copy(key, o, which):
        block = kbuf.at[key, o, c, which]
        return remote(block, block, csend.at[key, o, which], crecv.at[key, o, which], frame=mate)

    def cross_copy(key, o):
        block = kbuf.at[key, o, c, x]
        return remote(block, block, xsend.at[key, o], xrecv.at[key, o], frame=xmate)

    def await_block(block, sem):
        remote(block, block, csend.at[0, 0, 0], sem, frame=mate).wait_recv()

    def launch_own(key):
        near_copy(key).start()
        for i in range(R - 2):
            far_copy(key, i).start()
        half_copy(key, z).start()

    def take_near(key):
        await_block(kbuf.at[key, near, c], zrecv.at[key, near])
        half_copy(key, near).start()

    def take_far(key):
        for o in others:
            await_block(kbuf.at[key, o, c, x], zrecv.at[key, o])
            cross_copy(key, o).start()
            quarter_copy(key, o, x).start()

    def take_cross(key):
        for o in others:
            await_block(kbuf.at[key, o, c, 1 - x], xrecv.at[key, o])
            quarter_copy(key, o, 1 - x).start()

    def await_near(key):
        for o in (z, near):
            await_block(kbuf.at[key, o, 1 - c], crecv.at[key, o, 0])

    def await_far(key):
        for o in others:
            for which in range(2):
                await_block(kbuf.at[key, o, 1 - c, which], crecv.at[key, o, which])

    loads[0].wait()
    def query(tokens):
        q = dot(tokens.reshape(tokens.size // C, C), wq[...]).astype(BF16)
        return jnp.transpose(q * BF16(HEAD_DIM ** -0.5))

    q_ref[:, 0:M] = query(frames_ref[...])

    core_swap.wait_recv()
    current = jnp.where(lax.rem(owner, 2) == c, cand[c], corebuf[...])

    swaps = []
    for s in range(1, bits):
        bit = (me // 2 ** s) % 2
        partner = me + 2 ** s * (1 - 2 * bit)
        xsrc[s - 1] = current
        swap = remote(xsrc.at[s - 1], xdst.at[s - 1], bsend.at[s], brecv.at[s], frame=partner)
        swap.start()
        swaps.append(swap)
        if s == 1:

            @pl.when(me != F - 1)
            def _():
                await_block(kbuf.at[0, z, c], zrecv.at[0, z])

            launch_own(0)

            @pl.when(has_outer)
            def _():
                raw_copy.start()

        swap.wait_recv()
        current = jnp.where(lax.rem(lax.div(owner, 2 ** s), 2) == bit, current, xdst[s - 1])
    kbuf[1, z, c] = current
    launch_own(1)

    loads[1].wait()
    wvt[...] = jnp.transpose(wkv[:, C:])
    ones = jnp.ones((16, 2 * N), BF16)
    blank = jnp.zeros((HEAD_DIM, M), BF16)

    def project(key, chunk):
        pair = (z // 2 + chunk) % (R // 2)
        rows = kbuf[key, pl.ds(2 * pair, 2)].reshape(2 * N, C)
        k_ref[...] = dot(rows, wkv[:, :C]).astype(BF16)
        v = lax.dot_general(
            wvt[...], rows, (((1,), (1,)), ((), ())), preferred_element_type=F32
        )
        v_ref[...] = v.astype(BF16)

    def attend(rows):
        def two_heads(i, _):
            pair = pl.ds(pl.multiple_of(i * PAIR, PAIR), PAIR)
            kp = k_ref[:, pair]
            qp = q_ref[pair, rows]
            vp = v_ref[pair]
            for side in range(2):
                h = 2 * i + side
                own = pl.ds(pl.multiple_of(h * HEAD_DIM, HEAD_DIM), HEAD_DIM)
                half = slice(side * HEAD_DIM, (side + 1) * HEAD_DIM)
                qh = jnp.concatenate([blank, qp[half]] if side else [qp[half], blank], axis=0)
                scores = dot(kp, qh)
                before = m_ref[h, :, rows]
                top = jnp.maximum(jnp.max(scores, axis=0, keepdims=True), before)
                weights = jnp.exp(scores - top).astype(BF16)
                mixed = dot(jnp.concatenate([vp[half], ones], axis=0), weights)
                kept = jnp.exp(before - top)
                m_ref[h, :, rows] = top
                l_ref[h, :, rows] = l_ref[h, :, rows] * kept + mixed[HEAD_DIM : HEAD_DIM + 1]
                acc_ref[own, rows] = acc_ref[own, rows] * kept + mixed[:HEAD_DIM]
            return 0

        lax.fori_loop(0, HEADS // 2, two_heads, 0)

    m_ref[...] = jnp.full_like(m_ref, -1e30)
    l_ref[...] = jnp.zeros_like(l_ref)
    acc_ref[...] = jnp.zeros_like(acc_ref)
    halves = (slice(0, M), slice(M, 2 * M))

    def chunk(key, index):
        project(key, index)

        def block(i, _):
            attend(pl.ds(pl.multiple_of(i * M, M), M))
            return 0

        lax.fori_loop(0, 2, block, 0)

    chunks = R // 2
    take_near(0)
    await_near(0)
    project(0, 0)
    attend(halves[0])

    @pl.when(has_outer)
    def _():
        raw_copy.wait_recv()

    q_ref[:, M : M + 2 * N] = query(raw[...])
    take_far(0)
    take_near(1)
    attend(halves[1])
    await_near(1)
    chunk(1, 0)
    take_cross(0)
    take_far(1)
    await_far(0)
    for index in range(1, chunks):
        chunk(0, index)
    take_cross(1)
    await_far(1)
    for index in range(1, chunks - 1):
        chunk(1, index)
    project(1, chunks - 1)
    loads[2].wait()

    def finish(rows, tokens):
        count = rows.stop - rows.start
        attend(rows)
        for h in range(HEADS):
            own = slice(h * HEAD_DIM, (h + 1) * HEAD_DIM)
            att_ref[own, rows] = (acc_ref[own, rows] / l_ref[h, :, rows]).astype(BF16)
        res = tokens.reshape(count, C).astype(F32) + dot(
            jnp.transpose(att_ref[:, rows]), wo[...]
        )
        mean_square = jnp.mean(res * res, axis=-1, keepdims=True)
        gain = gain_ref[...].reshape(1, C)
        normed = (res * lax.rsqrt(mean_square + 1e-06) * gain).astype(BF16)
        return res.reshape(count // N, N, C), normed.reshape(count // N, N, C)

    res, normed = finish(halves[0], frames_ref[...])
    res_ref[...] = res
    nbuf[2 : T + 2] = normed
    inner_copy.start()
    _, normed = finish(halves[1], raw[...])
    nbuf[pl.ds(c * (T + 2), 2)] = jnp.where(has_outer, normed, jnp.zeros_like(normed))

    loads[3].wait()
    loads[4].wait()
    await_block(nbuf.at[pl.ds((1 - c) * (T + 2), 2)], hrecv.at[1])
    first = sum(dot(nbuf[j : j + T + 2].reshape(M + 2 * N, C), w1[j]) for j in range(3))
    hidden = first / (1.0 + jnp.exp(-first))
    hbuf[...] = hidden.astype(BF16).reshape(T + 2, N, C)

    @pl.when(me == 0)
    def _():
        hbuf[0] = jnp.zeros((N, C), BF16)

    @pl.when(me == F - 1)
    def _():
        hbuf[T + 1] = jnp.zeros((N, C), BF16)

    second = sum(dot(hbuf[j : j + T].reshape(M, C), w2[j]) for j in range(3))
    out_ref[...] = (res_ref[...] + second.reshape(T, N, C)).astype(BF16)

    @pl.when(me == F - 1)
    def _():
        for d in range(F - 1):
            last_copy(d).wait_send()

    core_swap.wait_send()
    for swap in swaps:
        swap.wait_send()
    for key in range(2):
        near_copy(key).wait_send()
        half_copy(key, z).wait_send()
        half_copy(key, near).wait_send()
        for i, o in enumerate(others):
            far_copy(key, i).wait_send()
            cross_copy(key, o).wait_send()
            for which in range(2):
                quarter_copy(key, o, which).wait_send()

    inner_copy.wait_send()

    @pl.when(has_outer)
    def _():
        raw_copy.wait_send()


def shards(F, R, frames, key_index, w_query, w_keyval, w_out, norm_gain, w_first, w_second):
    T, N, C = frames.shape
    Q, M = N // 4, T * N
    bits = F.bit_length() - 1
    assert F == 2 ** bits and F >= 4 and T == 2 and R % 2 == 0 and R >= 4
    vmem = pl.BlockSpec(memory_space=pltpu.VMEM)
    hbm = pl.BlockSpec(memory_space=pltpu.HBM)
    dma = pltpu.SemaphoreType.DMA
    out = pl.pallas_call(
        functools.partial(kernel, F, R),
        out_shape=jax.ShapeDtypeStruct((T, N, C), BF16),
        in_specs=[vmem, pl.BlockSpec(memory_space=pltpu.SMEM), vmem] + [hbm] * 5,
        out_specs=vmem,
        scratch_shapes=[
            pltpu.VMEM(w_query.shape, BF16),
            pltpu.VMEM(w_keyval.shape, BF16),
            pltpu.VMEM(w_out.shape, BF16),
            pltpu.VMEM(w_first.shape, BF16),
            pltpu.VMEM(w_second.shape, BF16),
            pltpu.VMEM((2, R, 2, 2, Q, C), BF16),
            pltpu.VMEM((2, 2, Q, C), BF16),
            pltpu.VMEM((2, Q, C), BF16),
            pltpu.VMEM((bits - 1, 2, Q, C), BF16),
            pltpu.VMEM((bits - 1, 2, Q, C), BF16),
            pltpu.VMEM((2, 2, 2, Q, C), BF16),
            pltpu.VMEM((C, C), BF16),
            pltpu.VMEM((C, M + 2 * N), BF16),
            pltpu.VMEM((2 * N, C), BF16),
            pltpu.VMEM((C, 2 * N), BF16),
            pltpu.VMEM((HEADS, 1, M + 2 * N), F32),
            pltpu.VMEM((HEADS, 1, M + 2 * N), F32),
            pltpu.VMEM((C, M + 2 * N), F32),
            pltpu.VMEM((C, M + 2 * N), BF16),
            pltpu.VMEM((T, N, C), F32),
            pltpu.VMEM((T + 4, N, C), BF16),
            pltpu.VMEM((T + 2, N, C), BF16),
            dma((5,)),
            dma((F - 1,)),
            dma((bits,)),
            dma((bits,)),
            dma((2, R - 1)),
            dma((2, R)),
            dma((2, R)),
            dma((2, R)),
            dma((2, R, 2)),
            dma((2, R, 2)),
            dma((2,)),
            dma((2,)),
        ],
        compiler_params=pltpu.CompilerParams(
            collective_id=0, has_side_effects=True, vmem_limit_bytes=60 * 2 ** 20
        ),
        cost_estimate=pl.CostEstimate(
            flops=5 * 10 ** 9, bytes_accessed=9 * 10 ** 6,
            transcendentals=M * 2 * R * N * HEADS,
        ),
    )(
        frames.reshape(T, 2, 2, Q, C), key_index, norm_gain,
        w_query, w_keyval, w_out, w_first, w_second,
    )
    return out


def solution(mesh):
    return jax.shard_map(
        functools.partial(shards, mesh.shape["frame"], mesh.shape["row"]),
        mesh=mesh,
        in_specs=(P(("clips", "frame"), "row", None), P("clips"), P(), P(), P(), P(), P(), P()),
        out_specs=P(("clips", "frame"), "row", None),
        check_vma=False,
    )
```

```python
import functools

import jax
import jax.numpy as jnp
from jax import lax
from jax.experimental import pallas as pl
from jax.experimental.pallas import tpu as pltpu
from jax.sharding import PartitionSpec as P

HEADS = 10
HEAD_DIM = 64
PAIR = 2 * HEAD_DIM
MESH = pl.DeviceIdType.MESH
F32 = jnp.float32
BF16 = jnp.bfloat16


def dot(a, b):
    return jnp.dot(a, b, preferred_element_type=F32)


def kernel(
    F, R,
    frames_ref, key_ref, gain_ref, wq_hbm, wkv_hbm, wo_hbm, w1_hbm, w2_hbm,
    out_ref,
    wq, wkv, wo, w1, w2, kbuf, cand, corebuf, xsrc, xdst, raw,
    wvt, q_ref, k_ref, v_ref, m_ref, l_ref, acc_ref, att_ref, res_ref, nbuf, hbuf,
    wsem, asend, bsend, brecv, zsend, zrecv, xsend, xrecv, csend, crecv, hsend, hrecv,
):
    T, _, _, Q, C = frames_ref.shape
    N = 4 * Q
    M = T * N
    me = lax.axis_index("frame")
    z = lax.axis_index("row")
    c = me % 2
    x = (me // 2) % 2
    mate = me + 1 - 2 * c
    xmate = me + 2 - 4 * x
    bits = F.bit_length() - 1
    outer = me + 2 * c - 1
    has_outer = (outer >= 0) & (outer < F)

    loads = [
        pltpu.make_async_copy(src, dst, wsem.at[i])
        for i, (src, dst) in enumerate(
            [(wq_hbm, wq), (wkv_hbm, wkv), (wo_hbm, wo), (w1_hbm, w1), (w2_hbm, w2)]
        )
    ]

    barrier = pltpu.get_barrier_semaphore()
    for step in range(1, F):
        pl.semaphore_signal(barrier, 1, device_id={"frame": (me + step) % F}, device_id_type=MESH)
    for step in range(1, R):
        pl.semaphore_signal(barrier, 1, device_id={"row": (z + step) % R}, device_id_type=MESH)
    for load in loads:
        load.start()

    other = key_ref[0] + key_ref[1] - (F * T - 1)
    owner = lax.div(other, T)
    local = lax.rem(other, T)
    chosen = frames_ref[0]
    for t in range(1, T):
        chosen = jnp.where(local == t, frames_ref[t], chosen)
    cand[...] = chosen

    @pl.when(me == F - 1)
    def _():
        kbuf[0, z, 1] = frames_ref[T - 1, 1]

    @pl.when((outer < 0) | (outer >= F))
    def _():
        raw[...] = jnp.zeros_like(raw)

    pl.semaphore_wait(barrier, F + R - 2)

    def remote(src, dst, ssem, rsem, **device):
        return pltpu.make_async_remote_copy(
            src_ref=src, dst_ref=dst, send_sem=ssem, recv_sem=rsem,
            device_id=device, device_id_type=MESH,
        )

    def last_copy(d):
        return remote(
            frames_ref.at[T - 1, d % 2], kbuf.at[0, z, d % 2],
            asend.at[d], zrecv.at[0, z], frame=d,
        )

    raw_copy = remote(
        frames_ref.at[pl.ds(c * (T - 2), 2)], raw, hsend.at[0], hrecv.at[0], frame=outer
    )
    inner_copy = remote(
        nbuf.at[pl.ds(2 + (1 - c) * (T - 2), 2)], nbuf.at[pl.ds(c * (T + 2), 2)],
        hsend.at[1], hrecv.at[1], frame=mate,
    )

    core_swap = remote(cand.at[1 - c], corebuf, bsend.at[0], brecv.at[0], frame=mate)
    core_swap.start()

    @pl.when(me == F - 1)
    def _():
        for d in range(F - 1):
            last_copy(d).start()

    near = z + 1 - 2 * (z % 2)
    others = [
        2 * ((z // 2 + step) % (R // 2)) + i for step in range(1, R // 2) for i in range(2)
    ]

    def near_copy(key):
        block = kbuf.at[key, z, c]
        return remote(block, block, zsend.at[key, 0], zrecv.at[key, z], row=near)

    def far_copy(key, i):
        block = kbuf.at[key, z, c, x]
        return remote(block, block, zsend.at[key, 1 + i], zrecv.at[key, z], row=others[i])

    def half_copy(key, o):
        block = kbuf.at[key, o, c]
        return remote(block, block, csend.at[key, o, 0], crecv.at[key, o, 0], frame=mate)

    def quarter_copy(key, o, which):
        block = kbuf.at[key, o, c, which]
        return remote(block, block, csend.at[key, o, which], crecv.at[key, o, which], frame=mate)

    def cross_copy(key, o):
        block = kbuf.at[key, o, c, x]
        return remote(block, block, xsend.at[key, o], xrecv.at[key, o], frame=xmate)

    def await_block(block, sem):
        remote(block, block, csend.at[0, 0, 0], sem, frame=mate).wait_recv()

    def launch_own(key):
        near_copy(key).start()
        for i in range(R - 2):
            far_copy(key, i).start()
        half_copy(key, z).start()

    def take_near(key):
        await_block(kbuf.at[key, near, c], zrecv.at[key, near])
        half_copy(key, near).start()

    def take_far(key):
        for o in others:
            await_block(kbuf.at[key, o, c, x], zrecv.at[key, o])
            cross_copy(key, o).start()
            quarter_copy(key, o, x).start()

    def take_cross(key):
        for o in others:
            await_block(kbuf.at[key, o, c, 1 - x], xrecv.at[key, o])
            quarter_copy(key, o, 1 - x).start()

    def await_near(key):
        for o in (z, near):
            await_block(kbuf.at[key, o, 1 - c], crecv.at[key, o, 0])

    def await_far(key):
        for o in others:
            for which in range(2):
                await_block(kbuf.at[key, o, 1 - c, which], crecv.at[key, o, which])

    loads[0].wait()
    def query(tokens):
        q = dot(tokens.reshape(tokens.size // C, C), wq[...]).astype(BF16)
        return jnp.transpose(q * BF16(HEAD_DIM ** -0.5))

    q_ref[:, 0:M] = query(frames_ref[...])

    core_swap.wait_recv()
    current = jnp.where(lax.rem(owner, 2) == c, cand[c], corebuf[...])

    swaps = []
    for s in range(1, bits):
        bit = (me // 2 ** s) % 2
        partner = me + 2 ** s * (1 - 2 * bit)
        xsrc[s - 1] = current
        swap = remote(xsrc.at[s - 1], xdst.at[s - 1], bsend.at[s], brecv.at[s], frame=partner)
        swap.start()
        swaps.append(swap)
        if s == 1:

            @pl.when(me != F - 1)
            def _():
                await_block(kbuf.at[0, z, c], zrecv.at[0, z])

            launch_own(0)

            @pl.when(has_outer)
            def _():
                raw_copy.start()

        swap.wait_recv()
        current = jnp.where(lax.rem(lax.div(owner, 2 ** s), 2) == bit, current, xdst[s - 1])
    kbuf[1, z, c] = current
    launch_own(1)

    loads[1].wait()
    wvt[...] = jnp.transpose(wkv[:, C:])
    ones = jnp.ones((16, 2 * N), BF16)
    blank = jnp.zeros((HEAD_DIM, M), BF16)

    def project(key, chunk):
        pair = (z // 2 + chunk) % (R // 2)
        rows = kbuf[key, pl.ds(2 * pair, 2)].reshape(2 * N, C)
        k_ref[...] = dot(rows, wkv[:, :C]).astype(BF16)
        v = lax.dot_general(
            wvt[...], rows, (((1,), (1,)), ((), ())), preferred_element_type=F32
        )
        v_ref[...] = v.astype(BF16)

    def attend(begin, end, rows):
        for h in range(HEADS):
            own = slice(h * HEAD_DIM, (h + 1) * HEAD_DIM)
            pair = slice(h // 2 * PAIR, (h // 2 + 1) * PAIR)
            qh = q_ref[own, rows]
            zero = blank[:, : qh.shape[1]]
            qh = jnp.concatenate([zero, qh] if h % 2 else [qh, zero], axis=0)
            scores = dot(k_ref[:, pair], qh)
            top = jnp.max(scores, axis=0, keepdims=True)
            if not begin:
                before = m_ref[h, :, rows]
                top = jnp.maximum(top, before)
            weights = jnp.exp(scores - top).astype(BF16)
            mixed = dot(jnp.concatenate([v_ref[own], ones], axis=0), weights)
            acc, low = mixed[:HEAD_DIM], mixed[HEAD_DIM : HEAD_DIM + 1]
            if not begin:
                kept = jnp.exp(before - top)
                acc = acc_ref[own, rows] * kept + acc
                low = l_ref[h, :, rows] * kept + low
            if end:
                att_ref[own, rows] = (acc / low).astype(BF16)
            else:
                m_ref[h, :, rows] = top
                l_ref[h, :, rows] = low
                acc_ref[own, rows] = acc

    halves = (slice(0, M), slice(M, M + 2 * N))

    def chunk(key, index, begin=False):
        project(key, index)
        for rows in halves:
            attend(begin, False, rows)

    chunks = R // 2
    take_near(0)
    await_near(0)
    project(0, 0)
    attend(True, False, halves[0])

    @pl.when(has_outer)
    def _():
        raw_copy.wait_recv()

    q_ref[:, M : M + 2 * N] = query(raw[...])
    take_far(0)
    take_near(1)
    attend(True, False, halves[1])
    await_near(1)
    chunk(1, 0)
    take_cross(0)
    take_far(1)
    await_far(0)
    for index in range(1, chunks):
        chunk(0, index)
    take_cross(1)
    await_far(1)
    for index in range(1, chunks - 1):
        chunk(1, index)
    project(1, chunks - 1)
    loads[2].wait()

    def finish(rows, tokens):
        count = rows.stop - rows.start
        attend(False, True, rows)
        res = tokens.reshape(count, C).astype(F32) + dot(
            jnp.transpose(att_ref[:, rows]), wo[...]
        )
        mean_square = jnp.mean(res * res, axis=-1, keepdims=True)
        gain = gain_ref[...].reshape(1, C)
        normed = (res * lax.rsqrt(mean_square + 1e-06) * gain).astype(BF16)
        return res.reshape(count // N, N, C), normed.reshape(count // N, N, C)

    res, normed = finish(halves[0], frames_ref[...])
    res_ref[...] = res
    nbuf[2 : T + 2] = normed
    inner_copy.start()
    _, normed = finish(halves[1], raw[...])
    nbuf[pl.ds(c * (T + 2), 2)] = jnp.where(has_outer, normed, jnp.zeros_like(normed))

    loads[3].wait()
    loads[4].wait()
    await_block(nbuf.at[pl.ds((1 - c) * (T + 2), 2)], hrecv.at[1])
    first = sum(dot(nbuf[j : j + T + 2].reshape(M + 2 * N, C), w1[j]) for j in range(3))
    hidden = first / (1.0 + jnp.exp(-first))
    hbuf[...] = hidden.astype(BF16).reshape(T + 2, N, C)

    @pl.when(me == 0)
    def _():
        hbuf[0] = jnp.zeros((N, C), BF16)

    @pl.when(me == F - 1)
    def _():
        hbuf[T + 1] = jnp.zeros((N, C), BF16)

    second = sum(dot(hbuf[j : j + T].reshape(M, C), w2[j]) for j in range(3))
    out_ref[...] = (res_ref[...] + second.reshape(T, N, C)).astype(BF16)

    @pl.when(me == F - 1)
    def _():
        for d in range(F - 1):
            last_copy(d).wait_send()

    core_swap.wait_send()
    for swap in swaps:
        swap.wait_send()
    for key in range(2):
        near_copy(key).wait_send()
        half_copy(key, z).wait_send()
        half_copy(key, near).wait_send()
        for i, o in enumerate(others):
            far_copy(key, i).wait_send()
            cross_copy(key, o).wait_send()
            for which in range(2):
                quarter_copy(key, o, which).wait_send()

    inner_copy.wait_send()

    @pl.when(has_outer)
    def _():
        raw_copy.wait_send()


def shards(F, R, frames, key_index, w_query, w_keyval, w_out, norm_gain, w_first, w_second):
    T, N, C = frames.shape
    Q, M = N // 4, T * N
    bits = F.bit_length() - 1
    assert F == 2 ** bits and F >= 4 and T >= 2 and R % 2 == 0 and R >= 4
    vmem = pl.BlockSpec(memory_space=pltpu.VMEM)
    hbm = pl.BlockSpec(memory_space=pltpu.HBM)
    dma = pltpu.SemaphoreType.DMA
    out = pl.pallas_call(
        functools.partial(kernel, F, R),
        out_shape=jax.ShapeDtypeStruct((T, N, C), BF16),
        in_specs=[vmem, pl.BlockSpec(memory_space=pltpu.SMEM), vmem] + [hbm] * 5,
        out_specs=vmem,
        scratch_shapes=[
            pltpu.VMEM(w_query.shape, BF16),
            pltpu.VMEM(w_keyval.shape, BF16),
            pltpu.VMEM(w_out.shape, BF16),
            pltpu.VMEM(w_first.shape, BF16),
            pltpu.VMEM(w_second.shape, BF16),
            pltpu.VMEM((2, R, 2, 2, Q, C), BF16),
            pltpu.VMEM((2, 2, Q, C), BF16),
            pltpu.VMEM((2, Q, C), BF16),
            pltpu.VMEM((bits - 1, 2, Q, C), BF16),
            pltpu.VMEM((bits - 1, 2, Q, C), BF16),
            pltpu.VMEM((2, 2, 2, Q, C), BF16),
            pltpu.VMEM((C, C), BF16),
            pltpu.VMEM((C, M + 2 * N), BF16),
            pltpu.VMEM((2 * N, C), BF16),
            pltpu.VMEM((C, 2 * N), BF16),
            pltpu.VMEM((HEADS, 1, M + 2 * N), F32),
            pltpu.VMEM((HEADS, 1, M + 2 * N), F32),
            pltpu.VMEM((C, M + 2 * N), F32),
            pltpu.VMEM((C, M + 2 * N), BF16),
            pltpu.VMEM((T, N, C), F32),
            pltpu.VMEM((T + 4, N, C), BF16),
            pltpu.VMEM((T + 2, N, C), BF16),
            dma((5,)),
            dma((F - 1,)),
            dma((bits,)),
            dma((bits,)),
            dma((2, R - 1)),
            dma((2, R)),
            dma((2, R)),
            dma((2, R)),
            dma((2, R, 2)),
            dma((2, R, 2)),
            dma((2,)),
            dma((2,)),
        ],
        compiler_params=pltpu.CompilerParams(
            collective_id=0, has_side_effects=True, vmem_limit_bytes=60 * 2 ** 20
        ),
        cost_estimate=pl.CostEstimate(
            flops=5 * 10 ** 9, bytes_accessed=9 * 10 ** 6,
            transcendentals=M * 2 * R * N * HEADS,
        ),
    )(
        frames.reshape(T, 2, 2, Q, C), key_index, norm_gain,
        w_query, w_keyval, w_out, w_first, w_second,
    )
    return out


def solution(mesh):
    return jax.shard_map(
        functools.partial(shards, mesh.shape["frame"], mesh.shape["row"]),
        mesh=mesh,
        in_specs=(P(("clips", "frame"), "row", None), P("clips"), P(), P(), P(), P(), P(), P()),
        out_specs=P(("clips", "frame"), "row", None),
        check_vma=False,
    )
```

```python
import functools

import jax
import jax.numpy as jnp
from jax import lax
from jax.experimental import pallas as pl
from jax.experimental.pallas import tpu as pltpu
from jax.sharding import PartitionSpec as P

HEADS = 10
HEAD_DIM = 64
PAIR = 2 * HEAD_DIM
MESH = pl.DeviceIdType.MESH
F32 = jnp.float32
BF16 = jnp.bfloat16


def dot(a, b):
    return jnp.dot(a, b, preferred_element_type=F32)


def kernel(
    F, R,
    frames_ref, key_ref, gain_ref, wq_hbm, wkv_hbm, wo_hbm, w1_hbm, w2_hbm,
    out_ref,
    wq, wkv, wo, w1, w2, kbuf, cand, corebuf, xsrc, xdst,
    q_ref, kv_ref, m_ref, l_ref, acc_ref, att_ref, res_ref, nbuf, hbuf, conv_ref, sum_ref,
    wsem, asend, bsend, brecv, zsend, zrecv, xsend, xrecv, csend, crecv, hsend, hrecv,
):
    T, _, _, Q, C = frames_ref.shape
    N = 4 * Q
    M = T * N
    me = lax.axis_index("frame")
    z = lax.axis_index("row")
    c = me % 2
    x = (me // 2) % 2
    mate = me + 1 - 2 * c
    xmate = me + 2 - 4 * x
    bits = F.bit_length() - 1

    loads = [
        pltpu.make_async_copy(src, dst, wsem.at[i])
        for i, (src, dst) in enumerate(
            [(wq_hbm, wq), (wkv_hbm, wkv), (wo_hbm, wo), (w1_hbm, w1), (w2_hbm, w2)]
        )
    ]

    barrier = pltpu.get_barrier_semaphore()
    for step in range(1, F):
        pl.semaphore_signal(barrier, 1, device_id={"frame": (me + step) % F}, device_id_type=MESH)
    for step in range(1, R):
        pl.semaphore_signal(barrier, 1, device_id={"row": (z + step) % R}, device_id_type=MESH)
    for load in loads:
        load.start()

    other = key_ref[0] + key_ref[1] - (F * T - 1)
    owner = lax.div(other, T)
    local = lax.rem(other, T)
    chosen = frames_ref[0]
    for t in range(1, T):
        chosen = jnp.where(local == t, frames_ref[t], chosen)
    cand[...] = chosen

    @pl.when(me == F - 1)
    def _():
        kbuf[0, z, 1] = frames_ref[T - 1, 1]

    pl.semaphore_wait(barrier, F + R - 2)

    def remote(src, dst, ssem, rsem, **device):
        return pltpu.make_async_remote_copy(
            src_ref=src, dst_ref=dst, send_sem=ssem, recv_sem=rsem,
            device_id=device, device_id_type=MESH,
        )

    def last_copy(d):
        return remote(
            frames_ref.at[T - 1, d % 2], kbuf.at[0, z, d % 2],
            asend.at[d], zrecv.at[0, z], frame=d,
        )

    core_swap = remote(cand.at[1 - c], corebuf, bsend.at[0], brecv.at[0], frame=mate)
    core_swap.start()

    @pl.when(me == F - 1)
    def _():
        for d in range(F - 1):
            last_copy(d).start()

    near = z + 1 - 2 * (z % 2)
    others = [
        2 * ((z // 2 + step) % (R // 2)) + i for step in range(1, R // 2) for i in range(2)
    ]

    def near_copy(key):
        block = kbuf.at[key, z, c]
        return remote(block, block, zsend.at[key, 0], zrecv.at[key, z], row=near)

    def far_copy(key, i):
        block = kbuf.at[key, z, c, x]
        return remote(block, block, zsend.at[key, 1 + i], zrecv.at[key, z], row=others[i])

    def half_copy(key, o):
        block = kbuf.at[key, o, c]
        return remote(block, block, csend.at[key, o, 0], crecv.at[key, o, 0], frame=mate)

    def quarter_copy(key, o, which):
        block = kbuf.at[key, o, c, which]
        return remote(block, block, csend.at[key, o, which], crecv.at[key, o, which], frame=mate)

    def cross_copy(key, o):
        block = kbuf.at[key, o, c, x]
        return remote(block, block, xsend.at[key, o], xrecv.at[key, o], frame=xmate)

    def await_block(block, sem):
        remote(block, block, csend.at[0, 0, 0], sem, frame=mate).wait_recv()

    def launch_own(key):
        near_copy(key).start()
        for i in range(R - 2):
            far_copy(key, i).start()
        half_copy(key, z).start()

    def take_near(key):
        await_block(kbuf.at[key, near, c], zrecv.at[key, near])
        half_copy(key, near).start()

    def take_far(key):
        for o in others:
            await_block(kbuf.at[key, o, c, x], zrecv.at[key, o])
            cross_copy(key, o).start()
            quarter_copy(key, o, x).start()

    def take_cross(key):
        for o in others:
            await_block(kbuf.at[key, o, c, 1 - x], xrecv.at[key, o])
            quarter_copy(key, o, 1 - x).start()

    def await_near(key):
        for o in (z, near):
            await_block(kbuf.at[key, o, 1 - c], crecv.at[key, o, 0])

    def await_far(key):
        for o in others:
            for which in range(2):
                await_block(kbuf.at[key, o, 1 - c, which], crecv.at[key, o, which])

    loads[0].wait()
    q = dot(frames_ref[...].reshape(M, C), wq[...]).astype(BF16)
    q_ref[...] = q * BF16(HEAD_DIM ** -0.5)

    core_swap.wait_recv()
    current = jnp.where(lax.rem(owner, 2) == c, cand[c], corebuf[...])

    swaps = []
    for s in range(1, bits):
        bit = (me // 2 ** s) % 2
        partner = me + 2 ** s * (1 - 2 * bit)
        xsrc[s - 1] = current
        swap = remote(xsrc.at[s - 1], xdst.at[s - 1], bsend.at[s], brecv.at[s], frame=partner)
        swap.start()
        swaps.append(swap)
        if s == 1:

            @pl.when(me != F - 1)
            def _():
                await_block(kbuf.at[0, z, c], zrecv.at[0, z])

            launch_own(0)
        swap.wait_recv()
        current = jnp.where(lax.rem(lax.div(owner, 2 ** s), 2) == bit, current, xdst[s - 1])
    kbuf[1, z, c] = current
    launch_own(1)

    loads[1].wait()
    lane = lax.broadcasted_iota(jnp.int32, (1, PAIR), 1)
    ones = jnp.ones((2 * N, PAIR), BF16)

    def project(key, chunk):
        pair = (z // 2 + chunk) % (R // 2)
        rows = kbuf[key, pl.ds(2 * pair, 2)].reshape(2 * N, C)
        kv_ref[...] = dot(rows, wkv[...]).astype(BF16)

    def attend(begin, end, rows, count):
        for i in range(HEADS // 2):
            cols = slice(i * PAIR, (i + 1) * PAIR)
            qp = q_ref[rows, cols]
            kp = kv_ref[:, cols]
            vp = jnp.concatenate([kv_ref[:, C + i * PAIR : C + (i + 1) * PAIR], ones], axis=1)
            blank = jnp.zeros_like(qp)
            qs = jnp.concatenate(
                [jnp.where(lane < HEAD_DIM, qp, blank), jnp.where(lane < HEAD_DIM, blank, qp)],
                axis=0,
            )
            scores = lax.dot_general(
                qs, kp, (((1,), (1,)), ((), ())), preferred_element_type=F32
            )
            top = jnp.max(scores, axis=-1, keepdims=True)
            weights = jnp.exp(scores - top).astype(BF16)
            mixed = dot(weights, vp)
            tops = jnp.broadcast_to(top, (2 * count, PAIR))
            parts = [
                (tops[part], mixed[part, PAIR:], mixed[part, :PAIR])
                for part in (slice(0, count), slice(count, 2 * count))
            ]
            top, low, acc = [jnp.where(lane < HEAD_DIM, a, b) for a, b in zip(*parts)]
            if not begin:
                before = m_ref[rows, cols]
                raised = jnp.maximum(before, top)
                old = jnp.exp(before - raised)
                new = jnp.exp(top - raised)
                acc = acc_ref[rows, cols] * old + acc * new
                low = l_ref[rows, cols] * old + low * new
                top = raised
            if end:
                att_ref[rows, cols] = (acc / low).astype(BF16)
            else:
                m_ref[rows, cols] = top
                l_ref[rows, cols] = low
                acc_ref[rows, cols] = acc

    everything = slice(0, M)
    chunks = R // 2
    take_near(0)
    await_near(0)
    project(0, 0)
    attend(True, False, everything, M)
    take_near(1)
    take_far(0)
    await_near(1)
    project(1, 0)
    attend(False, False, everything, M)
    take_cross(0)
    take_far(1)
    await_far(0)
    for chunk in range(1, chunks):
        project(0, chunk)
        attend(False, False, everything, M)
    take_cross(1)
    await_far(1)
    for chunk in range(1, chunks - 1):
        project(1, chunk)
        attend(False, False, everything, M)
    project(1, chunks - 1)

    def up_copy(f, piece):
        k, rows = f - (T - 2), pl.ds(piece * N // 2, N // 2)
        return remote(
            nbuf.at[2 + f, rows], nbuf.at[k, rows],
            hsend.at[0, f, piece], hrecv.at[0, k, piece], frame=(me + 1) % F,
        )

    def down_copy(f, piece):
        rows = pl.ds(piece * N // 2, N // 2)
        return remote(
            nbuf.at[2 + f, rows], nbuf.at[T + 2 + f, rows],
            hsend.at[1, f, piece], hrecv.at[1, f, piece], frame=(me + F - 1) % F,
        )

    def await_halo(side, slot, k):
        for piece in range(2):
            await_block(nbuf.at[slot, pl.ds(piece * N // 2, N // 2)], hrecv.at[side, k, piece])

    loads[2].wait()

    @pl.when(me == 0)
    def _():
        nbuf[0:2] = jnp.zeros((2, N, C), BF16)

    @pl.when(me == F - 1)
    def _():
        nbuf[T + 2 : T + 4] = jnp.zeros((2, N, C), BF16)

    for step in range(T):
        f = c * (T - 1 - step) + (1 - c) * step
        rows = pl.ds(pl.multiple_of(f * N, N), N)
        attend(False, True, rows, N)
        res = frames_ref[f].reshape(N, C).astype(F32) + dot(att_ref[rows, :], wo[...])
        res_ref[f] = res
        mean_square = jnp.mean(res * res, axis=-1, keepdims=True)
        gain = gain_ref[...].reshape(1, C)
        nbuf[2 + f] = (res * lax.rsqrt(mean_square + 1e-06) * gain).astype(BF16)

        @pl.when((me < F - 1) & (f >= T - 2))
        def _():
            for piece in range(2):
                up_copy(f, piece).start()

        @pl.when((me > 0) & (f < 2))
        def _():
            for piece in range(2):
                down_copy(f, piece).start()

    loads[3].wait()
    own = nbuf[2 : T + 2].reshape(M, C)
    for j in range(3):
        part = dot(own, w1[j]).reshape(T, N, C)
        if j == 0:
            conv_ref[0:2] = jnp.zeros((2, N, C), F32)
            conv_ref[2 : T + 2] = part
        else:
            conv_ref[2 - j : T + 2 - j] += part

    def exists(side):
        return ((side == 0) & (me > 0)) | ((side == 1) & (me < F - 1))

    sides = (1 - c, c)
    for side in sides:
        beside = 1 + side * (T + 1)

        @pl.when(exists(side))
        def _():
            await_halo(side, beside, 1 - side)

        halo = nbuf[beside]
        conv_ref[1 + side * (T - 1)] += dot(halo, w1[2 * side])
        conv_ref[side * (T + 1)] += dot(halo, w1[1])

    def silu(v):
        return v / (1.0 + jnp.exp(-v))

    hbuf[1 : T + 1] = silu(conv_ref[1 : T + 1]).astype(BF16)
    loads[4].wait()
    sum_ref[...] = res_ref[...] + dot(hbuf[1 : T + 1].reshape(M, C), w2[1]).reshape(T, N, C)
    inner = (T - 1) * N
    sum_ref[1:T] += dot(hbuf[1:T].reshape(inner, C), w2[0]).reshape(T - 1, N, C)
    sum_ref[0 : T - 1] += dot(hbuf[2 : T + 1].reshape(inner, C), w2[2]).reshape(T - 1, N, C)
    for side in sides:
        far = side * (T + 3)

        @pl.when(exists(side))
        def _():
            await_halo(side, far, side)

        value = conv_ref[side * (T + 1)] + dot(nbuf[far], w1[2 * side])
        keep = jnp.where(exists(side), 1.0, 0.0)
        outer = (silu(value) * keep).astype(BF16)
        edge = side * (T - 1)
        sum_ref[edge] += dot(outer, w2[2 * side])
    out_ref[...] = sum_ref[...].astype(BF16)

    @pl.when(me == F - 1)
    def _():
        for d in range(F - 1):
            last_copy(d).wait_send()

    core_swap.wait_send()
    for swap in swaps:
        swap.wait_send()
    for key in range(2):
        near_copy(key).wait_send()
        half_copy(key, z).wait_send()
        half_copy(key, near).wait_send()
        for i, o in enumerate(others):
            far_copy(key, i).wait_send()
            cross_copy(key, o).wait_send()
            for which in range(2):
                quarter_copy(key, o, which).wait_send()

    for f in range(T):

        @pl.when((me < F - 1) & (f >= T - 2))
        def _():
            for piece in range(2):
                up_copy(f, piece).wait_send()

        @pl.when((me > 0) & (f < 2))
        def _():
            for piece in range(2):
                down_copy(f, piece).wait_send()


def shards(F, R, frames, key_index, w_query, w_keyval, w_out, norm_gain, w_first, w_second):
    T, N, C = frames.shape
    Q, M = N // 4, T * N
    bits = F.bit_length() - 1
    assert F == 2 ** bits and F >= 4 and T >= 2 and R % 2 == 0 and R >= 4
    vmem = pl.BlockSpec(memory_space=pltpu.VMEM)
    any_space = pl.BlockSpec(memory_space=pl.ANY)
    dma = pltpu.SemaphoreType.DMA
    out = pl.pallas_call(
        functools.partial(kernel, F, R),
        out_shape=jax.ShapeDtypeStruct((T, N, C), BF16),
        in_specs=[vmem, pl.BlockSpec(memory_space=pltpu.SMEM), vmem] + [any_space] * 5,
        out_specs=vmem,
        scratch_shapes=[
            pltpu.VMEM(w_query.shape, BF16),
            pltpu.VMEM(w_keyval.shape, BF16),
            pltpu.VMEM(w_out.shape, BF16),
            pltpu.VMEM(w_first.shape, BF16),
            pltpu.VMEM(w_second.shape, BF16),
            pltpu.VMEM((2, R, 2, 2, Q, C), BF16),
            pltpu.VMEM((2, 2, Q, C), BF16),
            pltpu.VMEM((2, Q, C), BF16),
            pltpu.VMEM((bits - 1, 2, Q, C), BF16),
            pltpu.VMEM((bits - 1, 2, Q, C), BF16),
            pltpu.VMEM((M, C), BF16),
            pltpu.VMEM((2 * N, 2 * C), BF16),
            pltpu.VMEM((M, C), F32),
            pltpu.VMEM((M, C), F32),
            pltpu.VMEM((M, C), F32),
            pltpu.VMEM((M, C), BF16),
            pltpu.VMEM((T, N, C), F32),
            pltpu.VMEM((T + 4, N, C), BF16),
            pltpu.VMEM((T + 1, N, C), BF16),
            pltpu.VMEM((T + 2, N, C), F32),
            pltpu.VMEM((T, N, C), F32),
            dma((5,)),
            dma((F - 1,)),
            dma((bits,)),
            dma((bits,)),
            dma((2, R - 1)),
            dma((2, R)),
            dma((2, R)),
            dma((2, R)),
            dma((2, R, 2)),
            dma((2, R, 2)),
            dma((2, T, 2)),
            dma((2, 2, 2)),
        ],
        compiler_params=pltpu.CompilerParams(
            collective_id=0, has_side_effects=True, vmem_limit_bytes=60 * 2 ** 20
        ),
        cost_estimate=pl.CostEstimate(
            flops=5 * 10 ** 9, bytes_accessed=9 * 10 ** 6,
            transcendentals=M * 2 * R * N * HEADS,
        ),
    )(
        frames.reshape(T, 2, 2, Q, C), key_index, norm_gain,
        w_query, w_keyval, w_out, w_first, w_second,
    )
    return out


def solution(mesh):
    return jax.shard_map(
        functools.partial(shards, mesh.shape["frame"], mesh.shape["row"]),
        mesh=mesh,
        in_specs=(P(("clips", "frame"), "row", None), P("clips"), P(), P(), P(), P(), P(), P()),
        out_specs=P(("clips", "frame"), "row", None),
        check_vma=False,
    )
```
